512 devices in a mesh: seq: 128 (over z, x, core), head: 4 (over y).
Axes of the slice: x: 4, y: 4, z: 16, core: 2. Of those that a mesh axis runs over, the one named last changes fastest.
Arguments:
- queries: bfloat16 [32768, 512], P('seq', 'head'), may hold values from -16 to 16
- keys: bfloat16 [32768, 512], P('seq', 'head'), may hold values from -16 to 16
- values: bfloat16 [32768, 512], P('seq', 'head'), may hold values from -16 to 16
- out_weight: bfloat16 [512, 512], replicated, may hold values from -0.5 to 0.5
Outputs:
- mixed: bfloat16 [32768, 512], P(('seq', 'head'))
The draws below stay inside these ranges and needn't reach their ends.
All inputs are finite; a program needn't handle non-finite values.
Results may differ from the reference program's by a relative error of at most 0.00185.
The reference program's roundings to bfloat16 on the way count: a program that leaves them out, or rounds other values in their place, can miss the bound.
Values may be sent and summed in bfloat16 or wider, within the bound.
A program may use at most 128 MiB of HBM per device.

```python
import math
import jax
import jax.numpy as jnp
from jax import lax

D = 512
HEADS = 8
HD = 64
LEAF = 128
TOKENS = 32768


def multiscale(key):
    levels = TOKENS.bit_length() - 1
    coarse_weight = (0.5 / levels) ** 0.5
    summed = jnp.zeros((TOKENS, D), jnp.float32)
    for scale_index in range(levels + 1):
        count_rows = TOKENS >> scale_index
        subkey = jax.random.fold_in(key, scale_index)
        piece = jnp.clip(jax.random.normal(subkey, (count_rows, D), jnp.float32), -3.5, 3.5)
        factor = 0.5 ** 0.5 if scale_index == 0 else coarse_weight
        summed = summed + factor * jnp.repeat(piece, 2 ** scale_index, axis=0)
    return summed


def draw_queries(key, part):
    result = multiscale(jax.random.fold_in(key, 11))
    return result.astype(jnp.bfloat16)


def draw_keys(key, part):
    result = multiscale(jax.random.fold_in(key, 12))
    return result.astype(jnp.bfloat16)


def draw_values(key, part):
    return multiscale(jax.random.fold_in(key, 13)).astype(jnp.bfloat16)


def noise(key, shape, width, reach, kind=jnp.bfloat16):
    entries = jax.random.normal(key, shape, jnp.float32) * width
    return jnp.minimum(jnp.maximum(entries, -reach), reach).astype(kind)


def setup_inputs(seed: int = 0) -> dict:
    key_list = jax.random.split(jax.random.key(seed), 5)
    queries = draw_queries(jax.random.fold_in(key_list[4], 71), 0)
    keys = draw_keys(jax.random.fold_in(key_list[4], 71), 0)
    values = draw_values(jax.random.fold_in(key_list[4], 71), 0)
    out_weight = noise(key_list[3], (D, D), (D // 4) ** -0.5, 0.5)
    return {"queries": queries, "keys": keys, "values": values, "out_weight": out_weight}


def average_pairs(rows_in):
    widened = rows_in.astype(jnp.float32).reshape(rows_in.shape[0] // 2, 2, rows_in.shape[1])
    return (0.5 * (widened[:, 0] + widened[:, 1])).astype(jnp.bfloat16)

def reference(queries, keys, values, out_weight):
    block_count = TOKENS // LEAF
    top_level = block_count.bit_length() - 1
    level_keys = [keys]
    level_values = [values]
    for level in range(1, top_level):
        level_keys.append(average_pairs(level_keys[-1]))
        level_values.append(average_pairs(level_values[-1]))
    padded_keys = [jnp.pad(arr, ((LEAF, LEAF), (0, 0))) for arr in level_keys]
    padded_values = [jnp.pad(arr, ((LEAF, LEAF), (0, 0))) for arr in level_values]
    positions = jnp.arange(LEAF, dtype=jnp.int32)
    upper_half = positions >= LEAF // 2
    scale = 1.0 / math.sqrt(HD)

    def one_block(block):
        start = (block * LEAF).astype(jnp.int32)
        key_parts = [lax.dynamic_slice_in_dim(padded_keys[0], start, 3 * LEAF, 0)]
        value_parts = [lax.dynamic_slice_in_dim(padded_values[0], start, 3 * LEAF, 0)]
        neighbour = block - 1 + jnp.arange(3 * LEAF, dtype=jnp.int32) // LEAF
        valid_parts = [(neighbour >= 0) & (neighbour < block_count)]
        for level in range(1, top_level):
            coarse_block = block >> level
            parity = block >> level - 1 & 1
            level_blocks = block_count >> level
            lower_start = (coarse_block * LEAF).astype(jnp.int32)
            upper_start = ((coarse_block + 2) * LEAF).astype(jnp.int32)
            key_parts.append(lax.dynamic_slice_in_dim(padded_keys[level], lower_start, LEAF, 0))
            key_parts.append(lax.dynamic_slice_in_dim(padded_keys[level], upper_start, LEAF, 0))
            value_parts.append(lax.dynamic_slice_in_dim(padded_values[level], lower_start, LEAF, 0))
            value_parts.append(lax.dynamic_slice_in_dim(padded_values[level], upper_start, LEAF, 0))
            valid_parts.append((coarse_block >= 1) & jnp.logical_not(upper_half & (parity == 0)))
            valid_parts.append((coarse_block + 1 < level_blocks) & jnp.logical_not(jnp.logical_not(upper_half) & (parity == 1)))
        key_set = jnp.concatenate(key_parts, axis=0)
        value_set = jnp.concatenate(value_parts, axis=0)
        valid = jnp.concatenate(valid_parts, axis=0)
        query_rows = lax.dynamic_slice_in_dim(queries, start, LEAF, 0).astype(jnp.float32).reshape(LEAF, HEADS, HD)
        key_heads = key_set.astype(jnp.float32).reshape(-1, HEADS, HD)
        value_heads = value_set.astype(jnp.float32).reshape(-1, HEADS, HD)
        scores = jnp.einsum('qhd,khd->hqk', query_rows, key_heads) * scale
        scores = jnp.where(valid[None, None, :], scores, -jnp.inf)
        peak = lax.optimization_barrier(jnp.max(scores, axis=-1, keepdims=True))
        weights = jnp.exp(scores - peak)
        total = lax.optimization_barrier(jnp.sum(weights, axis=-1))
        rounded = lax.optimization_barrier(weights.astype(jnp.bfloat16)).astype(jnp.float32)
        numer = jnp.einsum('hqk,khd->hqd', rounded, value_heads)
        attended = (numer / total[..., None]).astype(jnp.bfloat16)
        return attended.transpose(1, 0, 2).reshape(LEAF, D)
    blocks = jnp.arange(block_count, dtype=jnp.int32)
    attended = lax.map(one_block, blocks, batch_size=4).reshape(TOKENS, D)
    return jnp.dot(attended, out_weight, preferred_element_type=jnp.float32).astype(jnp.bfloat16)
```

```python
import math

import jax
import jax.numpy as jnp
from jax import lax
from jax.experimental import pallas as pl
from jax.experimental.pallas import tpu as pltpu
from jax.sharding import PartitionSpec as P

MESH = pl.DeviceIdType.MESH
HD = 64
LEAF = 128
SPAN = 256
PLANE = 8
PLANES = 16
SEQ = PLANE * PLANES
HEADS_DEV = 4
NEAR, FAR = 1152, 512
COLS = NEAR + FAR
ROWS = 4 * LEAF
STRIP = 32
Z, N0, N1, L2, L3, L4, PL, AT, GROUPS = range(9)


def dot_t(a, b):
    return lax.dot_general(a, b, (((1,), (1,)), ((), ())), preferred_element_type=jnp.float32)


def dot(a, b):
    return jnp.dot(a, b, preferred_element_type=jnp.float32)


def pair_mean(rows):
    out = lax.broadcasted_iota(jnp.int32, (rows, 2 * rows), 0)
    inp = lax.broadcasted_iota(jnp.int32, (rows, 2 * rows), 1)
    return jnp.where((inp >> 1) == out, 0.5, 0.0).astype(jnp.bfloat16)


def group_mean(rows):
    out = lax.broadcasted_iota(jnp.int32, (rows, 2 * rows), 0)
    inp = lax.broadcasted_iota(jnp.int32, (rows, 2 * rows), 1)
    group = 2 * (out >> 4) + ((out >> 2) & 1)
    first = group * 16 + (out & 8) + 2 * (out & 3)
    return jnp.where((inp & ~1) == first, 0.5, 0.0).astype(jnp.bfloat16)


def open_if(valid):
    return jnp.where(valid, 0.0, -jnp.inf).astype(jnp.float32)


def bias_row(parts):
    total = sum(width for width, _ in parts)
    col = lax.broadcasted_iota(jnp.int32, (1, total), 1)
    row = jnp.zeros((1, total), jnp.float32)
    low = 0
    for width, value in parts:
        row = jnp.where((col >= low) & (col < low + width), value, row)
        low += width
    return row


def kernel(
    q_hbm, k_hbm, v_hbm, w_hbm, out_ref,
    q, kv, w, s1, s2, s3, s4, n0, n1, r2, r3, r4, zbuf, f5, f6, f7, pbuf,
    qm, scores, probs, total, att, gath,
    local_sem, send_sem, recv_sem,
):
    seq = lax.axis_index("seq")
    head = lax.axis_index("head")
    z = seq // PLANE
    r = seq % PLANE

    loads = [
        pltpu.make_async_copy(k_hbm, kv.at[0], local_sem.at[0]),
        pltpu.make_async_copy(v_hbm, kv.at[1], local_sem.at[1]),
        pltpu.make_async_copy(q_hbm, q, local_sem.at[2]),
        pltpu.make_async_copy(w_hbm, w, local_sem.at[3]),
    ]
    for load in loads:
        load.start()

    prev, following = (seq + SEQ - 1) % SEQ, (seq + 1) % SEQ

    def groups(size):
        index = seq // size
        odd = index % 2
        deltas = [-2, 2, 3 - 6 * odd]
        count = SEQ // size
        valid = [(index + d >= 0) & (index + d < count) for d in deltas]
        return [(index + d + count) % count for d in deltas], valid

    def members(size):
        pos = seq % size
        return [g * size + (pos ^ e) for g in groups(size)[0] for e in range(size)]

    planes = [((z + d) % PLANES) * PLANE + r for d in range(1, PLANES)]
    plane = [z * PLANE + (r ^ e) for e in range(1, PLANE)]
    two, three, four = members(1), members(2), members(4)
    heads = [head ^ e for e in range(1, HEADS_DEV)]

    barrier = pltpu.get_barrier_semaphore()
    met = [prev, following, *planes, *plane, *two, *three, *four]
    for t in met:
        pl.semaphore_signal(barrier, inc=1, device_id={"seq": t}, device_id_type=MESH)
    for t in heads:
        pl.semaphore_signal(barrier, inc=1, device_id={"head": t}, device_id_type=MESH)

    def send(src, dst, group, to):
        pltpu.make_async_remote_copy(
            src_ref=src, dst_ref=dst, send_sem=send_sem.at[group], recv_sem=recv_sem.at[group],
            device_id=to, device_id_type=MESH,
        ).start()

    def arrived(ref, group):
        pltpu.make_async_copy(ref, ref, recv_sem.at[group]).wait()

    def sent(ref, group):
        pltpu.make_async_copy(ref, ref, send_sem.at[group]).wait()

    loads[0].wait()
    loads[1].wait()
    both = jnp.concatenate([kv[0], kv[1]], axis=1)
    mean = pair_mean(LEAF)
    level = both
    for dst, rows in ((s1, 128), (s2, 64), (s3, 32), (s4, 16)):
        level = dot(mean[:rows, : 2 * rows], level).astype(jnp.bfloat16)
        dst[0] = level[:, :128]
        dst[1] = level[:, 128:]
    last = dot(mean[:8, :16], level)
    zbuf[z] = jnp.concatenate([last[:, :128], last[:, 128:]], axis=0).astype(jnp.bfloat16)

    pl.semaphore_wait(barrier, len(met) + len(heads))
    for t in planes:
        send(zbuf.at[z], zbuf.at[z], Z, {"seq": t})
    send(kv.at[:, pl.ds(LEAF, LEAF)], n0.at[0], N0, {"seq": following})
    send(kv.at[:, pl.ds(0, LEAF)], n0.at[1], N0, {"seq": prev})
    send(s1, n1.at[0], N1, {"seq": following})
    send(s1, n1.at[1], N1, {"seq": prev})
    def scatter(src, dst, group, targets):
        size = len(targets) // 3
        for i, t in enumerate(targets):
            slot = ((1, 0, 2)[i // size]) * size + i % size
            send(src, dst.at[slot], group, {"seq": t})

    scatter(s2, r2, L2, two)
    scatter(s3, r3, L3, three)
    scatter(s4, r4, L4, four)

    loads[2].wait()
    lane = lax.broadcasted_iota(jnp.int32, (LEAF, LEAF), 1)
    for leaf in range(2):
        block = q[leaf * LEAF : (leaf + 1) * LEAF] * jnp.bfloat16(1.0 / math.sqrt(HD))
        qm[leaf, :LEAF] = jnp.where(lane < HD, block, jnp.bfloat16(0))
        qm[leaf, LEAF:] = jnp.where(lane < HD, jnp.bfloat16(0), block)

    def put(leaf, low, keys, bias=None):
        part = dot_t(qm[leaf], keys)
        if bias is not None:
            part = part + bias
        scores[leaf * SPAN : (leaf + 1) * SPAN, low : low + keys.shape[0]] = part

    put(0, LEAF, kv[0])
    put(1, 0, kv[0])

    arrived(zbuf.at[pl.ds(0, PLANES - 1)], Z)
    fifth = zbuf[...].reshape(PLANES * 16, LEAF)
    f5[...] = fifth.astype(jnp.float32)
    mean = group_mean(LEAF)
    sixth = dot(mean, fifth).astype(jnp.bfloat16)
    f6[...] = sixth.astype(jnp.float32)
    f7[...] = dot(mean[:64, :128], sixth).astype(jnp.bfloat16).astype(jnp.float32)
    fifths, valid5 = groups(PLANE)
    sixths, valid6 = groups(2 * PLANE)
    seventh = z // 4
    step = 3 - 6 * (seventh % 2)
    sevenths = [(seventh + 2) % 4, (seventh + step + 4) % 4]
    valid7 = [None, (seventh + step >= 0) & (seventh + step < 4)]
    picks = [(f5, g) for g in fifths] + [(f6, g) for g in sixths] + [(f7, g) for g in sevenths]
    for side in range(2):
        rows = [ref[pl.ds(pl.multiple_of(g * 16 + side * 8, 8), 8), :] for ref, g in picks]
        pbuf[0, side] = jnp.concatenate(rows, axis=0).astype(jnp.bfloat16)
    for e, t in enumerate(plane):
        send(pbuf.at[0], pbuf.at[e + 1], PL, {"seq": t})

    has_prev, has_next = open_if(seq >= 1), open_if(seq + 1 < SEQ)
    bias2 = [(64, open_if(ok)) for ok in groups(1)[1]]
    bias34 = [(64, open_if(ok)) for size in (2, 4) for ok in groups(size)[1]]
    arrived(n0, N0)
    put(0, 0, n0[0, 0], has_prev)
    put(1, SPAN, n0[1, 0], has_next)
    arrived(n1, N1)
    arrived(r2, L2)
    second = r2[:, 0].reshape(192, LEAF)
    low_keys = jnp.concatenate([n1[0, 0, :64], n1[1, 0], second], axis=0)
    put(0, 384, low_keys, bias_row([(64, has_prev), (128, has_next), *bias2]))
    high_keys = jnp.concatenate([n1[0, 0], n1[1, 0, 64:], second], axis=0)
    put(1, 384, high_keys, bias_row([(128, has_prev), (64, has_next), *bias2]))
    arrived(r3, L3)
    arrived(r4, L4)
    keys = jnp.concatenate([r3[:, 0].reshape(192, LEAF), r4[:, 0].reshape(192, LEAF)], axis=0)
    row = bias_row(bias34)
    put(0, 768, keys, row)
    put(1, 768, keys, row)

    arrived(pbuf.at[pl.ds(0, PLANE - 1)], PL)
    col = lax.broadcasted_iota(jnp.int32, (1, FAR), 1)
    which = (col >> 3) & 7
    row = jnp.zeros((1, FAR), jnp.float32)
    for i, ok in enumerate([*valid5, *valid6, *valid7]):
        if ok is not None:
            row = jnp.where(which == i, open_if(ok), row)
    keys = pbuf[:, 0].reshape(FAR, LEAF)
    put(0, NEAR, keys, row)
    put(1, NEAR, keys, row)

    for low in range(0, ROWS, STRIP):
        strip = scores[low : low + STRIP]
        weights = jnp.exp(strip - jnp.max(strip, axis=1, keepdims=True))
        total[low : low + STRIP] = jnp.sum(weights, axis=1, keepdims=True)
        probs[low : low + STRIP] = weights.astype(jnp.bfloat16)

    second = r2[:, 1].reshape(192, LEAF)
    middle = jnp.concatenate([r3[:, 1].reshape(192, LEAF), r4[:, 1].reshape(192, LEAF)], axis=0)
    far = pbuf[:, 1].reshape(FAR, LEAF)
    near = (
        (n0[0, 1], kv[1], n1[0, 1, :64], n1[1, 1], second, middle, far),
        (kv[1], n0[1, 1], n1[0, 1], n1[1, 1, 64:], second, middle, far),
    )
    for leaf in range(2):
        rows = slice(leaf * SPAN, (leaf + 1) * SPAN)
        numer = dot(probs[rows], jnp.concatenate(near[leaf], axis=0))
        numer = numer / total[rows]
        rows_out = jnp.where(lane < HD, numer[:LEAF], numer[LEAF:]).astype(jnp.bfloat16)
        att[2 * leaf] = rows_out[:64]
        att[2 * leaf + 1] = rows_out[64:]

    gath[head] = att[head]
    for t in heads:
        send(att.at[t], gath.at[head], AT, {"head": t})
    loads[3].wait()
    arrived(gath.at[pl.ds(0, HEADS_DEV - 1)], AT)
    rows = jnp.concatenate([gath[i] for i in range(HEADS_DEV)], axis=1)
    out_ref[...] = dot(rows, w[...]).astype(jnp.bfloat16)

    sent(zbuf.at[pl.ds(0, PLANES - 1)], Z)
    sent(n0, N0)
    sent(n1, N1)
    sent(r2, L2)
    sent(r3, L3)
    sent(r4, L4)
    sent(pbuf.at[pl.ds(0, PLANE - 1)], PL)
    sent(gath.at[pl.ds(0, HEADS_DEV - 1)], AT)


def shards(queries, keys, values, out_weight):
    bf16, f32 = jnp.bfloat16, jnp.float32
    any_space = pl.BlockSpec(memory_space=pl.ANY)
    scratch = [
        ((SPAN, LEAF), bf16),
        ((2, SPAN, LEAF), bf16),
        ((512, 512), bf16),
        ((2, 128, LEAF), bf16),
        ((2, 64, LEAF), bf16),
        ((2, 32, LEAF), bf16),
        ((2, 16, LEAF), bf16),
        ((2, 2, LEAF, LEAF), bf16),
        ((2, 2, LEAF, LEAF), bf16),
        ((3, 2, 64, LEAF), bf16),
        ((6, 2, 32, LEAF), bf16),
        ((12, 2, 16, LEAF), bf16),
        ((PLANES, 16, LEAF), bf16),
        ((256, LEAF), f32),
        ((128, LEAF), f32),
        ((64, LEAF), f32),
        ((PLANE, 2, 64, LEAF), bf16),
        ((2, SPAN, LEAF), bf16),
        ((ROWS, COLS), f32),
        ((ROWS, COLS), bf16),
        ((ROWS, 1), f32),
        ((HEADS_DEV, 64, LEAF), bf16),
        ((HEADS_DEV, 64, LEAF), bf16),
    ]
    return pl.pallas_call(
        kernel,
        out_shape=jax.ShapeDtypeStruct((64, 512), bf16),
        in_specs=[any_space] * 4,
        out_specs=pl.BlockSpec(memory_space=pltpu.VMEM),
        scratch_shapes=[
            *(pltpu.VMEM(shape, kind) for shape, kind in scratch),
            pltpu.SemaphoreType.DMA((4,)),
            pltpu.SemaphoreType.DMA((GROUPS,)),
            pltpu.SemaphoreType.DMA((GROUPS,)),
        ],
        compiler_params=pltpu.CompilerParams(
            collective_id=0, has_side_effects=True, vmem_limit_bytes=40 * 2**20
        ),
    )(queries, keys, values, out_weight)


def solution(mesh):
    in_specs = (P("seq", "head"), P("seq", "head"), P("seq", "head"), P())
    out_specs = P(("seq", "head"), None)
    return jax.shard_map(shards, mesh=mesh, in_specs=in_specs, out_specs=out_specs, check_vma=False)
```

```python
import math

import jax
import jax.numpy as jnp
from jax import lax
from jax.experimental import pallas as pl
from jax.experimental.pallas import tpu as pltpu
from jax.sharding import PartitionSpec as P

MESH = pl.DeviceIdType.MESH
HD = 64
LEAF = 128
SPAN = 256
PLANE = 8
PLANES = 16
SEQ = PLANE * PLANES
HEADS_DEV = 4
NEAR, MID, FAR = 1152, 384, 128
COLS = NEAR + MID + FAR
EARLY = 4
ROWS = 4 * LEAF
STRIP = 32
N0, N1, L2, L3, L4, PM, PF, AT, Z5, Z6, Z7, GROUPS = 0, 2, 4, 7, 10, 13, 14, 15, 16, 19, 22, 24


def dot_t(a, b):
    return lax.dot_general(a, b, (((1,), (1,)), ((), ())), preferred_element_type=jnp.float32)


def dot(a, b):
    return jnp.dot(a, b, preferred_element_type=jnp.float32)


def pair_mean(rows):
    out = lax.broadcasted_iota(jnp.int32, (rows, 2 * rows), 0)
    inp = lax.broadcasted_iota(jnp.int32, (rows, 2 * rows), 1)
    return jnp.where((inp >> 1) == out, 0.5, 0.0).astype(jnp.bfloat16)


def group_mean(rows):
    out = lax.broadcasted_iota(jnp.int32, (rows, 2 * rows), 0)
    inp = lax.broadcasted_iota(jnp.int32, (rows, 2 * rows), 1)
    group = 2 * (out >> 4) + ((out >> 2) & 1)
    first = group * 16 + (out & 8) + 2 * (out & 3)
    return jnp.where((inp & ~1) == first, 0.5, 0.0).astype(jnp.bfloat16)


def open_if(valid):
    return jnp.where(valid, 0.0, -jnp.inf).astype(jnp.float32)


def bias_row(parts):
    total = sum(width for width, _ in parts)
    col = lax.broadcasted_iota(jnp.int32, (1, total), 1)
    row = jnp.zeros((1, total), jnp.float32)
    low = 0
    for width, value in parts:
        row = jnp.where((col >= low) & (col < low + width), value, row)
        low += width
    return row


def kernel(
    q_hbm, k_hbm, v_hbm, w_hbm, out_ref,
    q, kv, w, s1, s2, s3, s4, n0, n1, r2, r3, r4, zbuf, pmid, pfar,
    qm, scores, probs, total, att, gath,
    local_sem, send_sem, recv_sem, open_sem,
):
    seq = lax.axis_index("seq")
    head = lax.axis_index("head")
    z = seq // PLANE
    r = seq % PLANE

    loads = [
        pltpu.make_async_copy(k_hbm, kv.at[0], local_sem.at[0]),
        pltpu.make_async_copy(v_hbm, kv.at[1], local_sem.at[1]),
        pltpu.make_async_copy(q_hbm, q, local_sem.at[2]),
        pltpu.make_async_copy(w_hbm, w, local_sem.at[3]),
    ]
    for load in loads:
        load.start()

    def groups(size):
        index = seq // size
        odd = index % 2
        deltas = [-2, 2, 3 - 6 * odd]
        count = SEQ // size
        valid = [(index + d >= 0) & (index + d < count) for d in deltas]
        return [(index + d + count) % count for d in deltas], valid

    plane = [z * PLANE + (r ^ e) for e in (4, 5, 6, 7, 2, 3, 1)]
    heads = [head ^ e for e in (2, 1, 3)]

    zbuf[...] = jnp.zeros_like(zbuf)

    @pl.when((z == 0) | (z == PLANES - 1))
    def _():
        for ref in (n0, n1, r2, r3, r4):
            ref[...] = jnp.zeros_like(ref)

    def tell(sem, **to):
        pl.semaphore_signal(sem, inc=1, device_id=to, device_id_type=MESH)

    barrier = pltpu.get_barrier_semaphore()
    for d in (8, 7, 9, 6, 10, 5, 11, 4, 12, 3, 13, 2, 14, 15):
        pl.when(z + d < PLANES)(lambda d=d: tell(barrier, seq=seq + d * PLANE))
        pl.when((z - d >= 0) & (z - d < EARLY))(lambda d=d: tell(barrier, seq=seq - d * PLANE))
    for t in heads:
        tell(barrier, head=t)
    for t in plane:
        tell(barrier, seq=t)
    for d in (1, -1):

        @pl.when((z + d >= 0) & (z + d < PLANES))
        def _(d=d):
            for e in range(PLANE):
                tell(barrier, seq=(z + d) * PLANE + (r ^ e))

    above = (z + 1 < PLANES).astype(jnp.int32)
    below = (z > 0).astype(jnp.int32)
    partners = len(plane) + len(heads) + PLANE * (above + below)
    partners += jnp.where(z < EARLY, PLANES - 1 - above - below, z - below)

    def send(src, dst, group, to):
        pltpu.make_async_remote_copy(
            src_ref=src, dst_ref=dst, send_sem=send_sem.at[group], recv_sem=recv_sem.at[group],
            device_id=to, device_id_type=MESH,
        ).start()

    def arrived(ref, group):
        pltpu.make_async_copy(ref, ref, recv_sem.at[group]).wait()

    def sent(ref, group):
        pltpu.make_async_copy(ref, ref, send_sem.at[group]).wait()

    loads[0].wait()
    loads[1].wait()
    both = jnp.concatenate([kv[0], kv[1]], axis=1)
    mean = pair_mean(LEAF)
    level = both
    for dst, rows in ((s1, 128), (s2, 64), (s3, 32), (s4, 16)):
        level = dot(mean[:rows, : 2 * rows], level).astype(jnp.bfloat16)
        dst[0] = level[:, :128]
        dst[1] = level[:, 128:]
    last = dot(mean[:8, :16], level)
    zbuf[z] = jnp.concatenate([last[:, :128], last[:, 128:]], axis=0).astype(jnp.bfloat16)

    pl.semaphore_wait(barrier, partners)

    seventh = z // 4
    step = 3 - 6 * (seventh % 2)
    sevenths = [(seventh + 2) % 4, jnp.clip(seventh + step, 0, 3)]
    valid7 = [seventh >= 0, (seventh + step >= 0) & (seventh + step < 4)]
    (sixths, valid6), (fifths, valid5) = groups(2 * PLANE), groups(PLANE)
    classes = (
        (Z7, 4, sevenths, valid7, (0, 1)),
        (Z6, 2, sixths, valid6, (1, 0, 2)),
        (Z5, 1, fifths, valid5, (1, 0, 2)),
    )
    def each_group(ready):
        for group, size, others, valid, slots in classes:
            for i, (other, ok, slot) in enumerate(zip(others, valid, slots, strict=True)):
                targets = [(other * size + (z % size ^ e)) * PLANE + r for e in range(size)]

                def push(targets=targets, group=group, slot=slot):
                    for t in targets:
                        send(zbuf.at[z], zbuf.at[z], group + slot, {"seq": t})

                def admit(targets=targets, group=group, slot=slot):
                    for t in targets:
                        tell(open_sem.at[group - Z5 + slot], seq=t)

                def await_open(group=group, i=i, size=size):
                    pl.semaphore_wait(open_sem.at[group - Z5 + i], size)

                ready(ok, other * size, push, admit, await_open)

    def first_packets(ok, low, push, admit, await_open):
        pl.when(ok & ((low < z) | (z < EARLY)))(push)
        pl.when(ok & (low < z) & (low >= EARLY))(admit)

    def later_packets(ok, low, push, admit, await_open):
        @pl.when(ok & (low > z) & (z >= EARLY))
        def _():
            await_open()
            push()

    each_group(first_packets)

    def packets(wait, which):
        group, size, _, valid, slots = classes[which]
        for i, ok in enumerate(valid):
            slot = slots[i] if wait is sent else i
            pl.when(ok)(lambda slot=slot: wait(zbuf.at[pl.ds(0, size)], group + slot))

    def gathered(which):
        _, size, others, valid, _ = classes[which]
        picks = [jnp.where(ok, other, z // size) for other, ok in zip(others, valid, strict=True)]
        rows = [zbuf[pl.ds(g * size, size)].reshape(size * 16, LEAF) for g in picks]
        return jnp.concatenate(rows, axis=0)

    def forward(rows, dst, group):
        rows = rows.reshape(rows.shape[0] // 16, 2, 8, LEAF)
        for side in range(2):
            half = jnp.concatenate([rows[i, side] for i in range(rows.shape[0])], axis=0)
            dst[0, side] = half.astype(jnp.bfloat16)
        for e, t in enumerate(plane):
            send(dst.at[0], dst.at[e + 1], group, {"seq": t})

    has_prev, has_next = seq >= 1, seq + 1 < SEQ
    chain = ((L2, 1, s2, r2), (L3, 2, s3, r3), (L4, 4, s4, r4))

    @pl.when(has_next)
    def _():
        send(kv.at[:, pl.ds(LEAF, LEAF)], n0.at[0], N0, {"seq": seq + 1})
        send(s1, n1.at[0], N1, {"seq": seq + 1})

    @pl.when(has_prev)
    def _():
        send(kv.at[:, pl.ds(0, LEAF)], n0.at[1], N0 + 1, {"seq": seq - 1})
        send(s1, n1.at[1], N1 + 1, {"seq": seq - 1})

    for group, size, src, dst in chain:
        for i, (other, ok) in enumerate(zip(*groups(size), strict=True)):

            @pl.when(ok)
            def _(group=group, size=size, src=src, dst=dst, i=i, other=other):
                slot = (1, 0, 2)[i]
                for e in range(size):
                    to = other * size + (seq % size ^ e)
                    send(src, dst.at[slot * size + e], group + slot, {"seq": to})

    def near_done(wait, here, slots):
        for group, ref in ((N0, n0), (N1, n1)):
            pl.when(has_prev)(lambda group=group, ref=ref: wait(ref.at[0], group + here))
            pl.when(has_next)(lambda group=group, ref=ref: wait(ref.at[1], group + 1 - here))
        for group, size, _, dst in chain:
            for i, ok in enumerate(groups(size)[1]):
                k = slots[i]
                pl.when(ok)(lambda g=group, n=size, d=dst, k=k: wait(d.at[pl.ds(k * n, n)], g + k))

    loads[2].wait()
    lane = lax.broadcasted_iota(jnp.int32, (LEAF, LEAF), 1)
    for leaf in range(2):
        block = q[leaf * LEAF : (leaf + 1) * LEAF] * jnp.bfloat16(1.0 / math.sqrt(HD))
        qm[leaf, :LEAF] = jnp.where(lane < HD, block, jnp.bfloat16(0))
        qm[leaf, LEAF:] = jnp.where(lane < HD, jnp.bfloat16(0), block)

    def put(leaf, low, keys, bias=None):
        part = dot_t(qm[leaf], keys)
        if bias is not None:
            part = part + bias
        scores[leaf * SPAN : (leaf + 1) * SPAN, low : low + keys.shape[0]] = part

    put(0, LEAF, kv[0])
    put(1, 0, kv[0])

    each_group(later_packets)

    packets(arrived, 2)
    packets(arrived, 1)
    mean = group_mean(64)
    sixth = dot(mean[:48, :96], gathered(1))
    forward(jnp.concatenate([gathered(2).astype(jnp.float32), sixth], axis=0), pmid, PM)

    packets(arrived, 0)
    sixth = dot(mean, gathered(0)).astype(jnp.bfloat16)
    forward(dot(mean[:32, :64], sixth), pfar, PF)

    bias_prev, bias_next = open_if(has_prev), open_if(has_next)
    bias2 = [(64, open_if(ok)) for ok in groups(1)[1]]
    bias34 = [(64, open_if(ok)) for size in (2, 4) for ok in groups(size)[1]]
    near_done(arrived, 0, (0, 1, 2))
    put(0, 0, n0[0, 0], bias_prev)
    put(1, SPAN, n0[1, 0], bias_next)
    second = r2[:, 0].reshape(192, LEAF)
    low_keys = jnp.concatenate([n1[0, 0, :64], n1[1, 0], second], axis=0)
    put(0, 384, low_keys, bias_row([(64, bias_prev), (128, bias_next), *bias2]))
    high_keys = jnp.concatenate([n1[0, 0], n1[1, 0, 64:], second], axis=0)
    put(1, 384, high_keys, bias_row([(128, bias_prev), (64, bias_next), *bias2]))
    keys = jnp.concatenate([r3[:, 0].reshape(192, LEAF), r4[:, 0].reshape(192, LEAF)], axis=0)
    row = bias_row(bias34)
    put(0, 768, keys, row)
    put(1, 768, keys, row)

    biases = [(8, open_if(ok)) for ok in [*valid5, *valid6]]
    row = bias_row(biases * PLANE)
    arrived(pmid.at[pl.ds(0, PLANE - 1)], PM)
    keys = pmid[:, 0].reshape(MID, LEAF)
    put(0, NEAR, keys, row)
    put(1, NEAR, keys, row)
    row = bias_row([(8, open_if(ok)) for ok in valid7] * PLANE)
    arrived(pfar.at[pl.ds(0, PLANE - 1)], PF)
    keys = pfar[:, 0].reshape(FAR, LEAF)
    put(0, NEAR + MID, keys, row)
    put(1, NEAR + MID, keys, row)

    for low in range(0, ROWS, STRIP):
        strip = scores[low : low + STRIP]
        weights = jnp.exp(strip - jnp.max(strip, axis=1, keepdims=True))
        total[low : low + STRIP] = jnp.sum(weights, axis=1, keepdims=True)
        probs[low : low + STRIP] = weights.astype(jnp.bfloat16)

    second = r2[:, 1].reshape(192, LEAF)
    middle = jnp.concatenate([r3[:, 1].reshape(192, LEAF), r4[:, 1].reshape(192, LEAF)], axis=0)
    far = [pmid[:, 1].reshape(MID, LEAF), pfar[:, 1].reshape(FAR, LEAF)]
    near = (
        (n0[0, 1], kv[1], n1[0, 1, :64], n1[1, 1], second, middle, *far),
        (kv[1], n0[1, 1], n1[0, 1], n1[1, 1, 64:], second, middle, *far),
    )
    for leaf in range(2):
        rows = slice(leaf * SPAN, (leaf + 1) * SPAN)
        numer = dot(probs[rows], jnp.concatenate(near[leaf], axis=0))
        numer = numer / total[rows]
        rows_out = jnp.where(lane < HD, numer[:LEAF], numer[LEAF:]).astype(jnp.bfloat16)
        att[2 * leaf] = rows_out[:64]
        att[2 * leaf + 1] = rows_out[64:]

    gath[head] = att[head]
    for t in heads:
        send(att.at[t], gath.at[head], AT, {"head": t})
    loads[3].wait()
    arrived(gath.at[pl.ds(0, HEADS_DEV - 1)], AT)
    rows = jnp.concatenate([gath[i] for i in range(HEADS_DEV)], axis=1)
    out_ref[...] = dot(rows, w[...]).astype(jnp.bfloat16)

    for which in range(3):
        packets(sent, which)
    near_done(sent, 1, (1, 0, 2))
    sent(pmid.at[pl.ds(0, PLANE - 1)], PM)
    sent(pfar.at[pl.ds(0, PLANE - 1)], PF)
    sent(gath.at[pl.ds(0, HEADS_DEV - 1)], AT)


def shards(queries, keys, values, out_weight):
    bf16, f32 = jnp.bfloat16, jnp.float32
    hbm = pl.BlockSpec(memory_space=pltpu.HBM)
    scratch = [
        ((SPAN, LEAF), bf16),
        ((2, SPAN, LEAF), bf16),
        ((512, 512), bf16),
        ((2, 128, LEAF), bf16),
        ((2, 64, LEAF), bf16),
        ((2, 32, LEAF), bf16),
        ((2, 16, LEAF), bf16),
        ((2, 2, LEAF, LEAF), bf16),
        ((2, 2, LEAF, LEAF), bf16),
        ((3, 2, 64, LEAF), bf16),
        ((6, 2, 32, LEAF), bf16),
        ((12, 2, 16, LEAF), bf16),
        ((PLANES, 16, LEAF), bf16),
        ((PLANE, 2, 48, LEAF), bf16),
        ((PLANE, 2, 16, LEAF), bf16),
        ((2, SPAN, LEAF), bf16),
        ((ROWS, COLS), f32),
        ((ROWS, COLS), bf16),
        ((ROWS, 1), f32),
        ((HEADS_DEV, 64, LEAF), bf16),
        ((HEADS_DEV, 64, LEAF), bf16),
    ]
    return pl.pallas_call(
        kernel,
        out_shape=jax.ShapeDtypeStruct((64, 512), bf16),
        in_specs=[hbm] * 4,
        out_specs=pl.BlockSpec(memory_space=pltpu.VMEM),
        scratch_shapes=[
            *(pltpu.VMEM(shape, kind) for shape, kind in scratch),
            pltpu.SemaphoreType.DMA((4,)),
            pltpu.SemaphoreType.DMA((GROUPS,)),
            pltpu.SemaphoreType.DMA((GROUPS,)),
            pltpu.SemaphoreType.REGULAR((GROUPS - Z5,)),
        ],
        compiler_params=pltpu.CompilerParams(
            collective_id=0, has_side_effects=True, vmem_limit_bytes=63_400_000
        ),
    )(queries, keys, values, out_weight)


def solution(mesh):
    in_specs = (P("seq", "head"), P("seq", "head"), P("seq", "head"), P())
    out_specs = P(("seq", "head"), None)
    return jax.shard_map(shards, mesh=mesh, in_specs=in_specs, out_specs=out_specs, check_vma=False)
```

```python
import math

import jax
import jax.numpy as jnp
from jax import lax
from jax.experimental import pallas as pl
from jax.experimental.pallas import tpu as pltpu
from jax.sharding import PartitionSpec as P

MESH = pl.DeviceIdType.MESH
HD = 64
LEAF = 128
SPAN = 256
PLANE = 8
PLANES = 16
SEQ = PLANE * PLANES
HEADS_DEV = 4
NEAR, MID, FAR = 1152, 384, 128
COLS = NEAR + MID + FAR
ROWS = 4 * LEAF
STRIP = 32
N0, N1, L2, L3, L4, PM, PF, AT, Z5, Z6, Z7, GROUPS = 0, 2, 4, 7, 10, 13, 14, 15, 16, 19, 22, 24


def dot_t(a, b):
    return lax.dot_general(a, b, (((1,), (1,)), ((), ())), preferred_element_type=jnp.float32)


def dot(a, b):
    return jnp.dot(a, b, preferred_element_type=jnp.float32)


def pair_mean(rows):
    out = lax.broadcasted_iota(jnp.int32, (rows, 2 * rows), 0)
    inp = lax.broadcasted_iota(jnp.int32, (rows, 2 * rows), 1)
    return jnp.where((inp >> 1) == out, 0.5, 0.0).astype(jnp.bfloat16)


def group_mean(rows):
    out = lax.broadcasted_iota(jnp.int32, (rows, 2 * rows), 0)
    inp = lax.broadcasted_iota(jnp.int32, (rows, 2 * rows), 1)
    group = 2 * (out >> 4) + ((out >> 2) & 1)
    first = group * 16 + (out & 8) + 2 * (out & 3)
    return jnp.where((inp & ~1) == first, 0.5, 0.0).astype(jnp.bfloat16)


def open_if(valid):
    return jnp.where(valid, 0.0, -jnp.inf).astype(jnp.float32)


def bias_row(parts):
    total = sum(width for width, _ in parts)
    col = lax.broadcasted_iota(jnp.int32, (1, total), 1)
    row = jnp.zeros((1, total), jnp.float32)
    low = 0
    for width, value in parts:
        row = jnp.where((col >= low) & (col < low + width), value, row)
        low += width
    return row


def kernel(
    q_hbm, k_hbm, v_hbm, w_hbm, out_ref,
    q, kv, w, s1, s2, s3, s4, n0, n1, r2, r3, r4, zbuf, pmid, pfar,
    qm, scores, probs, total, att, gath,
    local_sem, send_sem, recv_sem, open_sem,
):
    seq = lax.axis_index("seq")
    head = lax.axis_index("head")
    z = seq // PLANE
    r = seq % PLANE

    loads = [
        pltpu.make_async_copy(k_hbm, kv.at[0], local_sem.at[0]),
        pltpu.make_async_copy(v_hbm, kv.at[1], local_sem.at[1]),
        pltpu.make_async_copy(q_hbm, q, local_sem.at[2]),
        pltpu.make_async_copy(w_hbm, w, local_sem.at[3]),
    ]
    for load in loads:
        load.start()

    def groups(size):
        index = seq // size
        odd = index % 2
        deltas = [-2, 2, 3 - 6 * odd]
        count = SEQ // size
        valid = [(index + d >= 0) & (index + d < count) for d in deltas]
        return [(index + d + count) % count for d in deltas], valid

    plane = [z * PLANE + (r ^ e) for e in (4, 5, 6, 7, 2, 3, 1)]
    heads = [head ^ e for e in (2, 1, 3)]

    zbuf[...] = jnp.zeros_like(zbuf)

    @pl.when((z == 0) | (z == PLANES - 1))
    def _():
        for ref in (n0, n1, r2, r3, r4):
            ref[...] = jnp.zeros_like(ref)

    def tell(sem, **to):
        pl.semaphore_signal(sem, inc=1, device_id=to, device_id_type=MESH)

    barrier = pltpu.get_barrier_semaphore()
    for d in (8, 7, 9, 6, 10, 5, 11, 4, 12, 3, 13, 2, 14, 15):
        pl.when(z + d < PLANES)(lambda d=d: tell(barrier, seq=seq + d * PLANE))
    for t in heads:
        tell(barrier, head=t)
    for t in plane:
        tell(barrier, seq=t)
    for d in (1, -1):

        @pl.when((z + d >= 0) & (z + d < PLANES))
        def _(d=d):
            for e in range(PLANE):
                tell(barrier, seq=(z + d) * PLANE + (r ^ e))

    above = (z + 1 < PLANES).astype(jnp.int32)
    below = (z > 0).astype(jnp.int32)
    partners = len(plane) + len(heads) + PLANE * (above + below) + z - below

    def send(src, dst, group, to):
        pltpu.make_async_remote_copy(
            src_ref=src, dst_ref=dst, send_sem=send_sem.at[group], recv_sem=recv_sem.at[group],
            device_id=to, device_id_type=MESH,
        ).start()

    def arrived(ref, group):
        pltpu.make_async_copy(ref, ref, recv_sem.at[group]).wait()

    def sent(ref, group):
        pltpu.make_async_copy(ref, ref, send_sem.at[group]).wait()

    loads[0].wait()
    loads[1].wait()
    both = jnp.concatenate([kv[0], kv[1]], axis=1)
    mean = pair_mean(LEAF)
    level = both
    for dst, rows in ((s1, 128), (s2, 64), (s3, 32), (s4, 16)):
        level = dot(mean[:rows, : 2 * rows], level).astype(jnp.bfloat16)
        dst[0] = level[:, :128]
        dst[1] = level[:, 128:]
    last = dot(mean[:8, :16], level)
    zbuf[z] = jnp.concatenate([last[:, :128], last[:, 128:]], axis=0).astype(jnp.bfloat16)

    pl.semaphore_wait(barrier, partners)

    seventh = z // 4
    step = 3 - 6 * (seventh % 2)
    sevenths = [(seventh + 2) % 4, jnp.clip(seventh + step, 0, 3)]
    valid7 = [seventh >= 0, (seventh + step >= 0) & (seventh + step < 4)]
    (sixths, valid6), (fifths, valid5) = groups(2 * PLANE), groups(PLANE)
    classes = (
        (Z7, 4, sevenths, valid7, (0, 1)),
        (Z6, 2, sixths, valid6, (1, 0, 2)),
        (Z5, 1, fifths, valid5, (1, 0, 2)),
    )
    def each_group(ready, chosen):
        for group, size, others, valid, slots in chosen:
            for i, (other, ok, slot) in enumerate(zip(others, valid, slots, strict=True)):
                targets = [(other * size + (z % size ^ e)) * PLANE + r for e in range(size)]

                def push(targets=targets, group=group, slot=slot):
                    for t in targets:
                        send(zbuf.at[z], zbuf.at[z], group + slot, {"seq": t})

                def admit(targets=targets, group=group, slot=slot):
                    for t in targets:
                        tell(open_sem.at[group - Z5 + slot], seq=t)

                def await_open(group=group, i=i, size=size):
                    pl.semaphore_wait(open_sem.at[group - Z5 + i], size)

                ready(ok, other * size, push, admit, await_open)

    def to_lower(ok, low, push, admit, await_open):
        @pl.when(ok & (low < z))
        def _():
            push()
            admit()

    def to_higher(ok, low, push, admit, await_open):
        @pl.when(ok & (low > z))
        def _():
            await_open()
            push()

    each_group(to_lower, classes)

    def packets(wait, which):
        group, size, _, valid, slots = classes[which]
        for i, ok in enumerate(valid):
            slot = slots[i] if wait is sent else i
            pl.when(ok)(lambda slot=slot: wait(zbuf.at[pl.ds(0, size)], group + slot))

    def gathered(which):
        _, size, others, valid, _ = classes[which]
        picks = [jnp.where(ok, other, z // size) for other, ok in zip(others, valid, strict=True)]
        rows = [zbuf[pl.ds(g * size, size)].reshape(size * 16, LEAF) for g in picks]
        return jnp.concatenate(rows, axis=0)

    def forward(rows, dst, group):
        rows = rows.reshape(rows.shape[0] // 16, 2, 8, LEAF)
        for side in range(2):
            half = jnp.concatenate([rows[i, side] for i in range(rows.shape[0])], axis=0)
            dst[0, side] = half.astype(jnp.bfloat16)
        for e, t in enumerate(plane):
            send(dst.at[0], dst.at[e + 1], group, {"seq": t})

    has_prev, has_next = seq >= 1, seq + 1 < SEQ
    chain = ((L2, 1, s2, r2), (L3, 2, s3, r3), (L4, 4, s4, r4))

    @pl.when(has_next)
    def _():
        send(kv.at[:, pl.ds(LEAF, LEAF)], n0.at[0], N0, {"seq": seq + 1})
        send(s1, n1.at[0], N1, {"seq": seq + 1})

    @pl.when(has_prev)
    def _():
        send(kv.at[:, pl.ds(0, LEAF)], n0.at[1], N0 + 1, {"seq": seq - 1})
        send(s1, n1.at[1], N1 + 1, {"seq": seq - 1})

    for group, size, src, dst in chain:
        for i, (other, ok) in enumerate(zip(*groups(size), strict=True)):

            @pl.when(ok)
            def _(group=group, size=size, src=src, dst=dst, i=i, other=other):
                slot = (1, 0, 2)[i]
                for e in range(size):
                    to = other * size + (seq % size ^ e)
                    send(src, dst.at[slot * size + e], group + slot, {"seq": to})

    def near_done(wait, here, slots):
        for group, ref in ((N0, n0), (N1, n1)):
            pl.when(has_prev)(lambda group=group, ref=ref: wait(ref.at[0], group + here))
            pl.when(has_next)(lambda group=group, ref=ref: wait(ref.at[1], group + 1 - here))
        for group, size, _, dst in chain:
            for i, ok in enumerate(groups(size)[1]):
                k = slots[i]
                pl.when(ok)(lambda g=group, n=size, d=dst, k=k: wait(d.at[pl.ds(k * n, n)], g + k))

    loads[2].wait()
    lane = lax.broadcasted_iota(jnp.int32, (LEAF, LEAF), 1)
    for leaf in range(2):
        block = q[leaf * LEAF : (leaf + 1) * LEAF] * jnp.bfloat16(1.0 / math.sqrt(HD))
        qm[leaf, :LEAF] = jnp.where(lane < HD, block, jnp.bfloat16(0))
        qm[leaf, LEAF:] = jnp.where(lane < HD, jnp.bfloat16(0), block)

    def put(leaf, low, keys, bias=None):
        part = dot_t(qm[leaf], keys)
        if bias is not None:
            part = part + bias
        scores[leaf * SPAN : (leaf + 1) * SPAN, low : low + keys.shape[0]] = part

    put(0, LEAF, kv[0])
    put(1, 0, kv[0])

    each_group(to_higher, (classes[2], classes[1], classes[0]))
    packets(arrived, 2)
    packets(arrived, 1)
    mean = group_mean(64)
    sixth = dot(mean[:48, :96], gathered(1))
    forward(jnp.concatenate([gathered(2).astype(jnp.float32), sixth], axis=0), pmid, PM)

    packets(arrived, 0)
    sixth = dot(mean, gathered(0)).astype(jnp.bfloat16)
    forward(dot(mean[:32, :64], sixth), pfar, PF)

    bias_prev, bias_next = open_if(has_prev), open_if(has_next)
    bias2 = [(64, open_if(ok)) for ok in groups(1)[1]]
    bias34 = [(64, open_if(ok)) for size in (2, 4) for ok in groups(size)[1]]
    near_done(arrived, 0, (0, 1, 2))
    put(0, 0, n0[0, 0], bias_prev)
    put(1, SPAN, n0[1, 0], bias_next)
    second = r2[:, 0].reshape(192, LEAF)
    low_keys = jnp.concatenate([n1[0, 0, :64], n1[1, 0], second], axis=0)
    put(0, 384, low_keys, bias_row([(64, bias_prev), (128, bias_next), *bias2]))
    high_keys = jnp.concatenate([n1[0, 0], n1[1, 0, 64:], second], axis=0)
    put(1, 384, high_keys, bias_row([(128, bias_prev), (64, bias_next), *bias2]))
    keys = jnp.concatenate([r3[:, 0].reshape(192, LEAF), r4[:, 0].reshape(192, LEAF)], axis=0)
    row = bias_row(bias34)
    put(0, 768, keys, row)
    put(1, 768, keys, row)

    biases = [(8, open_if(ok)) for ok in [*valid5, *valid6]]
    row = bias_row(biases * PLANE)
    arrived(pmid.at[pl.ds(0, PLANE - 1)], PM)
    keys = pmid[:, 0].reshape(MID, LEAF)
    put(0, NEAR, keys, row)
    put(1, NEAR, keys, row)
    row = bias_row([(8, open_if(ok)) for ok in valid7] * PLANE)
    arrived(pfar.at[pl.ds(0, PLANE - 1)], PF)
    keys = pfar[:, 0].reshape(FAR, LEAF)
    put(0, NEAR + MID, keys, row)
    put(1, NEAR + MID, keys, row)

    for low in range(0, ROWS, STRIP):
        strip = scores[low : low + STRIP]
        weights = jnp.exp(strip - jnp.max(strip, axis=1, keepdims=True))
        total[low : low + STRIP] = jnp.sum(weights, axis=1, keepdims=True)
        probs[low : low + STRIP] = weights.astype(jnp.bfloat16)

    second = r2[:, 1].reshape(192, LEAF)
    middle = jnp.concatenate([r3[:, 1].reshape(192, LEAF), r4[:, 1].reshape(192, LEAF)], axis=0)
    far = [pmid[:, 1].reshape(MID, LEAF), pfar[:, 1].reshape(FAR, LEAF)]
    near = (
        (n0[0, 1], kv[1], n1[0, 1, :64], n1[1, 1], second, middle, *far),
        (kv[1], n0[1, 1], n1[0, 1], n1[1, 1, 64:], second, middle, *far),
    )
    for leaf in range(2):
        rows = slice(leaf * SPAN, (leaf + 1) * SPAN)
        numer = dot(probs[rows], jnp.concatenate(near[leaf], axis=0))
        numer = numer / total[rows]
        rows_out = jnp.where(lane < HD, numer[:LEAF], numer[LEAF:]).astype(jnp.bfloat16)
        att[2 * leaf] = rows_out[:64]
        att[2 * leaf + 1] = rows_out[64:]

    gath[head] = att[head]
    for t in heads:
        send(att.at[t], gath.at[head], AT, {"head": t})
    loads[3].wait()
    arrived(gath.at[pl.ds(0, HEADS_DEV - 1)], AT)
    rows = jnp.concatenate([gath[i] for i in range(HEADS_DEV)], axis=1)
    out_ref[...] = dot(rows, w[...]).astype(jnp.bfloat16)

    for which in range(3):
        packets(sent, which)
    near_done(sent, 1, (1, 0, 2))
    sent(pmid.at[pl.ds(0, PLANE - 1)], PM)
    sent(pfar.at[pl.ds(0, PLANE - 1)], PF)
    sent(gath.at[pl.ds(0, HEADS_DEV - 1)], AT)


def shards(queries, keys, values, out_weight):
    bf16, f32 = jnp.bfloat16, jnp.float32
    hbm = pl.BlockSpec(memory_space=pltpu.HBM)
    scratch = [
        ((SPAN, LEAF), bf16),
        ((2, SPAN, LEAF), bf16),
        ((512, 512), bf16),
        ((2, 128, LEAF), bf16),
        ((2, 64, LEAF), bf16),
        ((2, 32, LEAF), bf16),
        ((2, 16, LEAF), bf16),
        ((2, 2, LEAF, LEAF), bf16),
        ((2, 2, LEAF, LEAF), bf16),
        ((3, 2, 64, LEAF), bf16),
        ((6, 2, 32, LEAF), bf16),
        ((12, 2, 16, LEAF), bf16),
        ((PLANES, 16, LEAF), bf16),
        ((PLANE, 2, 48, LEAF), bf16),
        ((PLANE, 2, 16, LEAF), bf16),
        ((2, SPAN, LEAF), bf16),
        ((ROWS, COLS), f32),
        ((ROWS, COLS), bf16),
        ((ROWS, 1), f32),
        ((HEADS_DEV, 64, LEAF), bf16),
        ((HEADS_DEV, 64, LEAF), bf16),
    ]
    return pl.pallas_call(
        kernel,
        out_shape=jax.ShapeDtypeStruct((64, 512), bf16),
        in_specs=[hbm] * 4,
        out_specs=pl.BlockSpec(memory_space=pltpu.VMEM),
        scratch_shapes=[
            *(pltpu.VMEM(shape, kind) for shape, kind in scratch),
            pltpu.SemaphoreType.DMA((4,)),
            pltpu.SemaphoreType.DMA((GROUPS,)),
            pltpu.SemaphoreType.DMA((GROUPS,)),
            pltpu.SemaphoreType.REGULAR((GROUPS - Z5,)),
        ],
        compiler_params=pltpu.CompilerParams(
            collective_id=0, has_side_effects=True, vmem_limit_bytes=63_400_000
        ),
    )(queries, keys, values, out_weight)


def solution(mesh):
    in_specs = (P("seq", "head"), P("seq", "head"), P("seq", "head"), P())
    out_specs = P(("seq", "head"), None)
    return jax.shard_map(shards, mesh=mesh, in_specs=in_specs, out_specs=out_specs, check_vma=False)
```

```python
import math

import jax
import jax.numpy as jnp
from jax import lax
from jax.experimental import pallas as pl
from jax.experimental.pallas import tpu as pltpu
from jax.sharding import PartitionSpec as P

MESH = pl.DeviceIdType.MESH
HD = 64
LEAF = 128
SPAN = 256
PLANE = 8
PLANES = 16
SEQ = PLANE * PLANES
HEADS_DEV = 4
NEAR, MID, FAR = 1152, 384, 128
COLS = NEAR + MID + FAR
ROWS = 4 * LEAF
STRIP = 32
N0, N1, L2, L3, L4, PM, PF, AT, Z5, Z6, Z7, GROUPS = 0, 2, 4, 7, 10, 13, 14, 15, 16, 19, 22, 24


def dot_t(a, b):
    return lax.dot_general(a, b, (((1,), (1,)), ((), ())), preferred_element_type=jnp.float32)


def dot(a, b):
    return jnp.dot(a, b, preferred_element_type=jnp.float32)


def pair_mean(rows):
    out = lax.broadcasted_iota(jnp.int32, (rows, 2 * rows), 0)
    inp = lax.broadcasted_iota(jnp.int32, (rows, 2 * rows), 1)
    return jnp.where((inp >> 1) == out, 0.5, 0.0).astype(jnp.bfloat16)


def group_mean(rows):
    out = lax.broadcasted_iota(jnp.int32, (rows, 2 * rows), 0)
    inp = lax.broadcasted_iota(jnp.int32, (rows, 2 * rows), 1)
    group = 2 * (out >> 4) + ((out >> 2) & 1)
    first = group * 16 + (out & 8) + 2 * (out & 3)
    return jnp.where((inp & ~1) == first, 0.5, 0.0).astype(jnp.bfloat16)


def open_if(valid):
    return jnp.where(valid, 0.0, -jnp.inf).astype(jnp.float32)


def bias_row(parts):
    total = sum(width for width, _ in parts)
    col = lax.broadcasted_iota(jnp.int32, (1, total), 1)
    row = jnp.zeros((1, total), jnp.float32)
    low = 0
    for width, value in parts:
        row = jnp.where((col >= low) & (col < low + width), value, row)
        low += width
    return row


def kernel(
    q_hbm, k_hbm, v_hbm, w_hbm, out_ref,
    q, kv, w, s1, s2, s3, s4, n0, n1, r2, r3, r4, zbuf, pmid, pfar,
    qm, scores, probs, total, att, gath,
    local_sem, send_sem, recv_sem, open_sem, open_near, open_head,
):
    seq = lax.axis_index("seq")
    head = lax.axis_index("head")
    z = seq // PLANE
    r = seq % PLANE

    loads = [
        pltpu.make_async_copy(k_hbm, kv.at[0], local_sem.at[0]),
        pltpu.make_async_copy(v_hbm, kv.at[1], local_sem.at[1]),
        pltpu.make_async_copy(q_hbm, q, local_sem.at[2]),
        pltpu.make_async_copy(w_hbm, w, local_sem.at[3]),
    ]
    for load in loads:
        load.start()

    def groups(size):
        index = seq // size
        odd = index % 2
        deltas = [-2, 2, 3 - 6 * odd]
        count = SEQ // size
        valid = [(index + d >= 0) & (index + d < count) for d in deltas]
        return [(index + d + count) % count for d in deltas], valid

    plane = [z * PLANE + (r ^ e) for e in (4, 5, 6, 7, 2, 3, 1)]
    heads = [head ^ e for e in (2, 1, 3)]

    zbuf[...] = jnp.zeros_like(zbuf)

    @pl.when((z == 0) | (z == PLANES - 1))
    def _():
        for ref in (n0, n1, r2, r3, r4):
            ref[...] = jnp.zeros_like(ref)

    def rank(place):
        return (place >> 1 ^ place >> 2) * 2 + (place & 1)

    def tell(sem, **to):
        pl.semaphore_signal(sem, inc=1, device_id=to, device_id_type=MESH)

    barrier = pltpu.get_barrier_semaphore()
    for d in (8, 7, 9, 6, 10, 5, 11, 4, 12, 3, 13, 2, 14, 15):
        pl.when(z + d < PLANES)(lambda d=d: tell(barrier, seq=seq + d * PLANE))
    mine, mine_head = rank(r), head ^ head >> 1
    above = (z + 1 < PLANES).astype(jnp.int32)
    below = (z > 0).astype(jnp.int32)

    def greet(later, near, heads_sem):
        def chosen(a, b):
            return a < b if later else a > b

        for t in heads:
            pl.when(chosen(mine_head, t ^ t >> 1))(lambda t=t: tell(heads_sem, head=t))
        for d in (0, 1, -1):
            for e in range(1, PLANE):
                place = r ^ e

                if d == 0 and e == 1:
                    if later:
                        tell(near, seq=seq ^ 1)
                    continue

                @pl.when((z + d >= 0) & (z + d < PLANES) & chosen(mine, rank(place)))
                def _(d=d, place=place):
                    tell(near, seq=(z + d) * PLANE + place)

        d = 1 if later else -1
        pl.when((z + d >= 0) & (z + d < PLANES))(lambda: tell(near, seq=seq + d * PLANE))

    greet(True, barrier, barrier)

    def send(src, dst, group, to):
        pltpu.make_async_remote_copy(
            src_ref=src, dst_ref=dst, send_sem=send_sem.at[group], recv_sem=recv_sem.at[group],
            device_id=to, device_id_type=MESH,
        ).start()

    def arrived(ref, group):
        pltpu.make_async_copy(ref, ref, recv_sem.at[group]).wait()

    def sent(ref, group):
        pltpu.make_async_copy(ref, ref, send_sem.at[group]).wait()

    loads[0].wait()
    loads[1].wait()
    both = jnp.concatenate([kv[0], kv[1]], axis=1)
    mean = pair_mean(LEAF)
    level = both
    for dst, rows in ((s1, 128), (s2, 64), (s3, 32), (s4, 16)):
        level = dot(mean[:rows, : 2 * rows], level).astype(jnp.bfloat16)
        dst[0] = level[:, :128]
        dst[1] = level[:, 128:]
    last = dot(mean[:8, :16], level)
    zbuf[z] = jnp.concatenate([last[:, :128], last[:, 128:]], axis=0).astype(jnp.bfloat16)

    core = seq % 2
    pl.semaphore_wait(barrier, mine * (1 + above + below) - core + 1 + z + mine_head)

    seventh = z // 4
    step = 3 - 6 * (seventh % 2)
    sevenths = [(seventh + 2) % 4, jnp.clip(seventh + step, 0, 3)]
    valid7 = [seventh >= 0, (seventh + step >= 0) & (seventh + step < 4)]
    (sixths, valid6), (fifths, valid5) = groups(2 * PLANE), groups(PLANE)
    classes = (
        (Z7, 4, sevenths, valid7, (0, 1)),
        (Z6, 2, sixths, valid6, (1, 0, 2)),
        (Z5, 1, fifths, valid5, (1, 0, 2)),
    )
    def each_group(ready, chosen):
        for group, size, others, valid, slots in chosen:
            for i, (other, ok, slot) in enumerate(zip(others, valid, slots, strict=True)):
                targets = [(other * size + (z % size ^ e)) * PLANE + r for e in range(size)]

                def push(targets=targets, group=group, slot=slot):
                    for t in targets:
                        send(zbuf.at[z], zbuf.at[z], group + slot, {"seq": t})

                def admit(targets=targets, group=group, slot=slot):
                    for t in targets:
                        tell(open_sem.at[group - Z5 + slot], seq=t)

                def await_open(group=group, i=i, size=size):
                    pl.semaphore_wait(open_sem.at[group - Z5 + i], size)

                ready(ok, other * size, push, admit, await_open)

    def to_lower(ok, low, push, admit, await_open):
        @pl.when(ok & (low < z))
        def _():
            push()
            admit()

    def to_higher(ok, low, push, admit, await_open):
        @pl.when(ok & (low > z))
        def _():
            await_open()
            push()

    each_group(to_lower, classes)
    greet(False, open_near, open_head)

    def packets(wait, which):
        group, size, _, valid, slots = classes[which]
        for i, ok in enumerate(valid):
            slot = slots[i] if wait is sent else i
            pl.when(ok)(lambda slot=slot: wait(zbuf.at[pl.ds(0, size)], group + slot))

    def gathered(which):
        _, size, others, valid, _ = classes[which]
        picks = [jnp.where(ok, other, z // size) for other, ok in zip(others, valid, strict=True)]
        rows = [zbuf[pl.ds(g * size, size)].reshape(size * 16, LEAF) for g in picks]
        return jnp.concatenate(rows, axis=0)

    def forward(rows, dst, group):
        rows = rows.reshape(rows.shape[0] // 16, 2, 8, LEAF)
        for side in range(2):
            half = jnp.concatenate([rows[i, side] for i in range(rows.shape[0])], axis=0)
            dst[0, side] = half.astype(jnp.bfloat16)
        for e, t in enumerate(plane):
            send(dst.at[0], dst.at[e + 1], group, {"seq": t})

    later_near = (PLANE - 1 - mine) * (1 + above + below) - 1 + core + above
    pl.when(later_near > 0)(lambda: pl.semaphore_wait(open_near, later_near))

    has_prev, has_next = seq >= 1, seq + 1 < SEQ
    chain = ((L2, 1, s2, r2), (L3, 2, s3, r3), (L4, 4, s4, r4))

    @pl.when(has_next)
    def _():
        send(kv.at[:, pl.ds(LEAF, LEAF)], n0.at[0], N0, {"seq": seq + 1})
        send(s1, n1.at[0], N1, {"seq": seq + 1})

    @pl.when(has_prev)
    def _():
        send(kv.at[:, pl.ds(0, LEAF)], n0.at[1], N0 + 1, {"seq": seq - 1})
        send(s1, n1.at[1], N1 + 1, {"seq": seq - 1})

    for group, size, src, dst in chain:
        for i, (other, ok) in enumerate(zip(*groups(size), strict=True)):

            @pl.when(ok)
            def _(group=group, size=size, src=src, dst=dst, i=i, other=other):
                slot = (1, 0, 2)[i]
                for e in range(size):
                    to = other * size + (seq % size ^ e)
                    send(src, dst.at[slot * size + e], group + slot, {"seq": to})

    def near_done(wait, here, slots):
        for group, ref in ((N0, n0), (N1, n1)):
            pl.when(has_prev)(lambda group=group, ref=ref: wait(ref.at[0], group + here))
            pl.when(has_next)(lambda group=group, ref=ref: wait(ref.at[1], group + 1 - here))
        for group, size, _, dst in chain:
            for i, ok in enumerate(groups(size)[1]):
                k = slots[i]
                pl.when(ok)(lambda g=group, n=size, d=dst, k=k: wait(d.at[pl.ds(k * n, n)], g + k))

    loads[2].wait()
    lane = lax.broadcasted_iota(jnp.int32, (LEAF, LEAF), 1)
    for leaf in range(2):
        block = q[leaf * LEAF : (leaf + 1) * LEAF] * jnp.bfloat16(1.0 / math.sqrt(HD))
        qm[leaf, :LEAF] = jnp.where(lane < HD, block, jnp.bfloat16(0))
        qm[leaf, LEAF:] = jnp.where(lane < HD, jnp.bfloat16(0), block)

    def put(leaf, low, keys, bias=None):
        part = dot_t(qm[leaf], keys)
        if bias is not None:
            part = part + bias
        scores[leaf * SPAN : (leaf + 1) * SPAN, low : low + keys.shape[0]] = part

    put(0, LEAF, kv[0])
    put(1, 0, kv[0])

    each_group(to_higher, (classes[2], classes[1], classes[0]))
    packets(arrived, 2)
    packets(arrived, 1)
    mean = group_mean(64)
    sixth = dot(mean[:48, :96], gathered(1))
    forward(jnp.concatenate([gathered(2).astype(jnp.float32), sixth], axis=0), pmid, PM)

    packets(arrived, 0)
    sixth = dot(mean, gathered(0)).astype(jnp.bfloat16)
    forward(dot(mean[:32, :64], sixth), pfar, PF)

    bias_prev, bias_next = open_if(has_prev), open_if(has_next)
    bias2 = [(64, open_if(ok)) for ok in groups(1)[1]]
    bias34 = [(64, open_if(ok)) for size in (2, 4) for ok in groups(size)[1]]
    near_done(arrived, 0, (0, 1, 2))
    put(0, 0, n0[0, 0], bias_prev)
    put(1, SPAN, n0[1, 0], bias_next)
    second = r2[:, 0].reshape(192, LEAF)
    low_keys = jnp.concatenate([n1[0, 0, :64], n1[1, 0], second], axis=0)
    put(0, 384, low_keys, bias_row([(64, bias_prev), (128, bias_next), *bias2]))
    high_keys = jnp.concatenate([n1[0, 0], n1[1, 0, 64:], second], axis=0)
    put(1, 384, high_keys, bias_row([(128, bias_prev), (64, bias_next), *bias2]))
    keys = jnp.concatenate([r3[:, 0].reshape(192, LEAF), r4[:, 0].reshape(192, LEAF)], axis=0)
    row = bias_row(bias34)
    put(0, 768, keys, row)
    put(1, 768, keys, row)

    biases = [(8, open_if(ok)) for ok in [*valid5, *valid6]]
    row = bias_row(biases * PLANE)
    arrived(pmid.at[pl.ds(0, PLANE - 1)], PM)
    keys = pmid[:, 0].reshape(MID, LEAF)
    put(0, NEAR, keys, row)
    put(1, NEAR, keys, row)
    row = bias_row([(8, open_if(ok)) for ok in valid7] * PLANE)
    arrived(pfar.at[pl.ds(0, PLANE - 1)], PF)
    keys = pfar[:, 0].reshape(FAR, LEAF)
    put(0, NEAR + MID, keys, row)
    put(1, NEAR + MID, keys, row)

    second = r2[:, 1].reshape(192, LEAF)
    middle = jnp.concatenate([r3[:, 1].reshape(192, LEAF), r4[:, 1].reshape(192, LEAF)], axis=0)
    far = [pmid[:, 1].reshape(MID, LEAF), pfar[:, 1].reshape(FAR, LEAF)]
    near = (
        (n0[0, 1], kv[1], n1[0, 1, :64], n1[1, 1], second, middle, *far),
        (kv[1], n0[1, 1], n1[0, 1], n1[1, 1, 64:], second, middle, *far),
    )
    later_heads = HEADS_DEV - 1 - mine_head
    pl.when(later_heads > 0)(lambda: pl.semaphore_wait(open_head, later_heads))
    for leaf in range(2):
        rows = slice(leaf * SPAN, (leaf + 1) * SPAN)
        for low in range(leaf * SPAN, (leaf + 1) * SPAN, STRIP):
            strip = scores[low : low + STRIP]
            weights = jnp.exp(strip - jnp.max(strip, axis=1, keepdims=True))
            total[low : low + STRIP] = jnp.sum(weights, axis=1, keepdims=True)
            probs[low : low + STRIP] = weights.astype(jnp.bfloat16)
        numer = dot(probs[rows], jnp.concatenate(near[leaf], axis=0))
        numer = numer / total[rows]
        rows_out = jnp.where(lane < HD, numer[:LEAF], numer[LEAF:]).astype(jnp.bfloat16)
        att[2 * leaf] = rows_out[:64]
        att[2 * leaf + 1] = rows_out[64:]
        for to in (2 * leaf, 2 * leaf + 1):
            pl.when(head != to)(lambda to=to: send(att.at[to], gath.at[head], AT, {"head": to}))

    gath[head] = att[head]
    loads[3].wait()
    arrived(gath.at[pl.ds(0, HEADS_DEV - 1)], AT)
    rows = jnp.concatenate([gath[i] for i in range(HEADS_DEV)], axis=1)
    out_ref[...] = dot(rows, w[...]).astype(jnp.bfloat16)

    for which in range(3):
        packets(sent, which)
    near_done(sent, 1, (1, 0, 2))
    sent(pmid.at[pl.ds(0, PLANE - 1)], PM)
    sent(pfar.at[pl.ds(0, PLANE - 1)], PF)
    sent(gath.at[pl.ds(0, HEADS_DEV - 1)], AT)


def shards(queries, keys, values, out_weight):
    bf16, f32 = jnp.bfloat16, jnp.float32
    hbm = pl.BlockSpec(memory_space=pltpu.HBM)
    scratch = [
        ((SPAN, LEAF), bf16),
        ((2, SPAN, LEAF), bf16),
        ((512, 512), bf16),
        ((2, 128, LEAF), bf16),
        ((2, 64, LEAF), bf16),
        ((2, 32, LEAF), bf16),
        ((2, 16, LEAF), bf16),
        ((2, 2, LEAF, LEAF), bf16),
        ((2, 2, LEAF, LEAF), bf16),
        ((3, 2, 64, LEAF), bf16),
        ((6, 2, 32, LEAF), bf16),
        ((12, 2, 16, LEAF), bf16),
        ((PLANES, 16, LEAF), bf16),
        ((PLANE, 2, 48, LEAF), bf16),
        ((PLANE, 2, 16, LEAF), bf16),
        ((2, SPAN, LEAF), bf16),
        ((ROWS, COLS), f32),
        ((ROWS, COLS), bf16),
        ((ROWS, 1), f32),
        ((HEADS_DEV, 64, LEAF), bf16),
        ((HEADS_DEV, 64, LEAF), bf16),
    ]
    return pl.pallas_call(
        kernel,
        out_shape=jax.ShapeDtypeStruct((64, 512), bf16),
        in_specs=[hbm] * 4,
        out_specs=pl.BlockSpec(memory_space=pltpu.VMEM),
        scratch_shapes=[
            *(pltpu.VMEM(shape, kind) for shape, kind in scratch),
            pltpu.SemaphoreType.DMA((4,)),
            pltpu.SemaphoreType.DMA((GROUPS,)),
            pltpu.SemaphoreType.DMA((GROUPS,)),
            pltpu.SemaphoreType.REGULAR((GROUPS - Z5,)),
            pltpu.SemaphoreType.REGULAR,
            pltpu.SemaphoreType.REGULAR,
        ],
        compiler_params=pltpu.CompilerParams(
            collective_id=0, has_side_effects=True, vmem_limit_bytes=63_400_000
        ),
    )(queries, keys, values, out_weight)


def solution(mesh):
    in_specs = (P("seq", "head"), P("seq", "head"), P("seq", "head"), P())
    out_specs = P(("seq", "head"), None)
    return jax.shard_map(shards, mesh=mesh, in_specs=in_specs, out_specs=out_specs, check_vma=False)
```

```python
import math

import jax
import jax.numpy as jnp
from jax import lax
from jax.experimental import pallas as pl
from jax.experimental.pallas import tpu as pltpu
from jax.sharding import PartitionSpec as P

MESH = pl.DeviceIdType.MESH
HD = 64
LEAF = 128
SPAN = 256
PLANE = 8
PLANES = 16
SEQ = PLANE * PLANES
HEADS_DEV = 4
NEAR, MID, FAR = 1152, 384, 128
COLS = NEAR + MID + FAR
ROWS = 4 * LEAF
STRIP = 32
N0, N1, L2, L3, L4, PM, PF, AT, Z5, Z6, Z7, GROUPS = 0, 2, 4, 7, 10, 13, 14, 15, 16, 19, 22, 24


def dot_t(a, b):
    return lax.dot_general(a, b, (((1,), (1,)), ((), ())), preferred_element_type=jnp.float32)


def dot(a, b):
    return jnp.dot(a, b, preferred_element_type=jnp.float32)


def pair_mean(rows):
    out = lax.broadcasted_iota(jnp.int32, (rows, 2 * rows), 0)
    inp = lax.broadcasted_iota(jnp.int32, (rows, 2 * rows), 1)
    return jnp.where((inp >> 1) == out, 0.5, 0.0).astype(jnp.bfloat16)


def group_mean(rows):
    out = lax.broadcasted_iota(jnp.int32, (rows, 2 * rows), 0)
    inp = lax.broadcasted_iota(jnp.int32, (rows, 2 * rows), 1)
    group = 2 * (out >> 4) + ((out >> 2) & 1)
    first = group * 16 + (out & 8) + 2 * (out & 3)
    return jnp.where((inp & ~1) == first, 0.5, 0.0).astype(jnp.bfloat16)


def open_if(valid):
    return jnp.where(valid, 0.0, -jnp.inf).astype(jnp.float32)


def bias_row(parts):
    total = sum(width for width, _ in parts)
    col = lax.broadcasted_iota(jnp.int32, (1, total), 1)
    row = jnp.zeros((1, total), jnp.float32)
    low = 0
    for width, value in parts:
        row = jnp.where((col >= low) & (col < low + width), value, row)
        low += width
    return row


def kernel(
    q_hbm, k_hbm, v_hbm, w_hbm, out_ref,
    q, kv, w, s1, s2, s3, s4, n0, n1, r2, r3, r4, zbuf, pmid, pfar,
    qm, scores, probs, total, att, gath,
    local_sem, send_sem, recv_sem, open_sem, open_near, open_head,
):
    seq = lax.axis_index("seq")
    head = lax.axis_index("head")
    z = seq // PLANE
    r = seq % PLANE

    loads = [
        pltpu.make_async_copy(k_hbm, kv.at[0], local_sem.at[0]),
        pltpu.make_async_copy(v_hbm, kv.at[1], local_sem.at[1]),
        pltpu.make_async_copy(q_hbm, q, local_sem.at[2]),
        pltpu.make_async_copy(w_hbm, w, local_sem.at[3]),
    ]
    for load in loads:
        load.start()

    def groups(size):
        index = seq // size
        odd = index % 2
        deltas = [-2, 2, 3 - 6 * odd]
        count = SEQ // size
        valid = [(index + d >= 0) & (index + d < count) for d in deltas]
        return [(index + d + count) % count for d in deltas], valid

    plane = [z * PLANE + (r ^ e) for e in (4, 5, 6, 7, 2, 3, 1)]
    heads = [head ^ e for e in (2, 1, 3)]

    zbuf[...] = jnp.zeros_like(zbuf)
    pmid[:, 2] = jnp.zeros_like(pmid[:, 2])

    @pl.when((z == 0) | (z == PLANES - 1))
    def _():
        for ref in (n0, n1, r2, r3, r4):
            ref[...] = jnp.zeros_like(ref)

    def rank(place):
        return (place >> 1 ^ place >> 2) * 2 + (place & 1)

    def tell(sem, **to):
        pl.semaphore_signal(sem, inc=1, device_id=to, device_id_type=MESH)

    barrier = pltpu.get_barrier_semaphore()
    for d in (8, 7, 9, 6, 10, 5, 11, 4, 12, 3, 13, 2, 14, 15):
        pl.when(z + d < PLANES)(lambda d=d: tell(barrier, seq=seq + d * PLANE))
    mine, mine_head = rank(r), head ^ head >> 1
    above = (z + 1 < PLANES).astype(jnp.int32)
    below = (z > 0).astype(jnp.int32)

    def greet(later, near, heads_sem):
        def chosen(a, b):
            return a < b if later else a > b

        for t in heads:
            pl.when(chosen(mine_head, t ^ t >> 1))(lambda t=t: tell(heads_sem, head=t))
        for d in (0, 1, -1):
            for e in range(1, PLANE):
                place = r ^ e

                if d == 0 and e == 1:
                    if later:
                        tell(near, seq=seq ^ 1)
                    continue

                @pl.when((z + d >= 0) & (z + d < PLANES) & chosen(mine, rank(place)))
                def _(d=d, place=place):
                    tell(near, seq=(z + d) * PLANE + place)

        d = 1 if later else -1
        pl.when((z + d >= 0) & (z + d < PLANES))(lambda: tell(near, seq=seq + d * PLANE))

    greet(True, barrier, barrier)

    def send(src, dst, group, to):
        pltpu.make_async_remote_copy(
            src_ref=src, dst_ref=dst, send_sem=send_sem.at[group], recv_sem=recv_sem.at[group],
            device_id=to, device_id_type=MESH,
        ).start()

    def arrived(ref, group):
        pltpu.make_async_copy(ref, ref, recv_sem.at[group]).wait()

    def sent(ref, group):
        pltpu.make_async_copy(ref, ref, send_sem.at[group]).wait()

    loads[0].wait()
    loads[1].wait()
    both = jnp.concatenate([kv[0], kv[1]], axis=1)
    mean = pair_mean(LEAF)
    level = both
    for dst, rows in ((s1, 128), (s2, 64), (s3, 32), (s4, 16)):
        level = dot(mean[:rows, : 2 * rows], level).astype(jnp.bfloat16)
        dst[0] = level[:, :128]
        dst[1] = level[:, 128:]
    last = dot(mean[:8, :16], level)
    zbuf[z] = jnp.concatenate([last[:, :128], last[:, 128:]], axis=0).astype(jnp.bfloat16)

    core = seq % 2
    pl.semaphore_wait(barrier, mine * (1 + above + below) - core + 1 + z + mine_head)

    seventh = z // 4
    step = 3 - 6 * (seventh % 2)
    sevenths = [(seventh + 2) % 4, jnp.clip(seventh + step, 0, 3)]
    valid7 = [seventh >= 0, (seventh + step >= 0) & (seventh + step < 4)]
    low_half = z < PLANES // 2

    def existing_first(size):
        (a, b, c), (is_a, is_b, is_c) = groups(size)
        pick = lambda low, high: jnp.where(low_half, low, high)
        others, valid = [pick(b, a), c, pick(a, b)], [pick(is_b, is_a), is_c, pick(is_a, is_b)]
        return others, valid

    (sixths, valid6), (fifths, valid5) = existing_first(2 * PLANE), existing_first(PLANE)
    one = low_half.astype(jnp.int32)
    here, there = (one, 2, 1 - one), (1 - one, 2, one)
    classes = (
        (Z7, 4, sevenths, valid7, (0, 1), (0, 1)),
        (Z6, 2, sixths, valid6, here, there),
        (Z5, 1, fifths, valid5, here, there),
    )
    def each_group(ready, chosen):
        for group, size, others, valid, places, slots in chosen:
            for other, ok, i, slot in zip(others, valid, places, slots, strict=True):
                targets = [(other * size + (z % size ^ e)) * PLANE + r for e in range(size)]

                def push(targets=targets, group=group, slot=slot):
                    for t in targets:
                        send(zbuf.at[z], zbuf.at[z], group + slot, {"seq": t})

                def admit(targets=targets, group=group, slot=slot):
                    for t in targets:
                        tell(open_sem.at[group - Z5 + slot], seq=t)

                def await_open(group=group, i=i, size=size):
                    pl.semaphore_wait(open_sem.at[group - Z5 + i], size)

                ready(ok, other * size, push, admit, await_open)

    def to_lower(ok, low, push, admit, await_open):
        @pl.when(ok & (low < z))
        def _():
            push()
            admit()

    def to_higher(ok, low, push, admit, await_open):
        @pl.when(ok & (low > z))
        def _():
            await_open()
            push()

    each_group(to_lower, classes)
    greet(False, open_near, open_head)

    def packets(wait, which):
        group, size, _, valid, places, slots = classes[which]
        for ok, slot in zip(valid, slots if wait is sent else places, strict=True):
            pl.when(ok)(lambda slot=slot: wait(zbuf.at[pl.ds(0, size)], group + slot))

    def gathered(which):
        _, size, others, valid, _, _ = classes[which]
        picks = [jnp.where(ok, other, z // size) for other, ok in zip(others, valid, strict=True)]
        rows = [zbuf[pl.ds(g * size, size)].reshape(size * 16, LEAF) for g in picks]
        return jnp.concatenate(rows, axis=0)

    def forward(blocks, dst):
        for side in range(2):
            half = slice(side * 8, side * 8 + 8)
            dst[side] = jnp.concatenate([block[half] for block in blocks], axis=0).astype(jnp.bfloat16)

    ends = (z < 2) | (z >= PLANES - 2)

    def middle_blocks(wait):
        pl.when(ends)(lambda: wait(pmid.at[pl.ds(0, PLANE - 1), pl.ds(0, 2)], PM))
        pl.when(jnp.logical_not(ends))(lambda: wait(pmid.at[pl.ds(0, PLANE - 1)], PM))

    later_near = (PLANE - 1 - mine) * (1 + above + below) - 1 + core + above
    pl.when(later_near > 0)(lambda: pl.semaphore_wait(open_near, later_near))

    has_prev, has_next = seq >= 1, seq + 1 < SEQ
    chain = ((L2, 1, s2, r2), (L3, 2, s3, r3), (L4, 4, s4, r4))

    @pl.when(has_next)
    def _():
        send(kv.at[:, pl.ds(LEAF, LEAF)], n0.at[0], N0, {"seq": seq + 1})
        send(s1, n1.at[0], N1, {"seq": seq + 1})

    @pl.when(has_prev)
    def _():
        send(kv.at[:, pl.ds(0, LEAF)], n0.at[1], N0 + 1, {"seq": seq - 1})
        send(s1, n1.at[1], N1 + 1, {"seq": seq - 1})

    for group, size, src, dst in chain:
        for i, (other, ok) in enumerate(zip(*groups(size), strict=True)):

            @pl.when(ok)
            def _(group=group, size=size, src=src, dst=dst, i=i, other=other):
                slot = (1, 0, 2)[i]
                for e in range(size):
                    to = other * size + (seq % size ^ e)
                    send(src, dst.at[slot * size + e], group + slot, {"seq": to})

    def near_done(wait, here, slots):
        for group, ref in ((N0, n0), (N1, n1)):
            pl.when(has_prev)(lambda group=group, ref=ref: wait(ref.at[0], group + here))
            pl.when(has_next)(lambda group=group, ref=ref: wait(ref.at[1], group + 1 - here))
        for group, size, _, dst in chain:
            for i, ok in enumerate(groups(size)[1]):
                k = slots[i]
                pl.when(ok)(lambda g=group, n=size, d=dst, k=k: wait(d.at[pl.ds(k * n, n)], g + k))

    loads[2].wait()
    lane = lax.broadcasted_iota(jnp.int32, (LEAF, LEAF), 1)
    for leaf in range(2):
        block = q[leaf * LEAF : (leaf + 1) * LEAF] * jnp.bfloat16(1.0 / math.sqrt(HD))
        qm[leaf, :LEAF] = jnp.where(lane < HD, block, jnp.bfloat16(0))
        qm[leaf, LEAF:] = jnp.where(lane < HD, jnp.bfloat16(0), block)

    def put(leaf, low, keys, bias=None):
        part = dot_t(qm[leaf], keys)
        if bias is not None:
            part = part + bias
        scores[leaf * SPAN : (leaf + 1) * SPAN, low : low + keys.shape[0]] = part

    put(0, LEAF, kv[0])
    put(1, 0, kv[0])

    each_group(to_higher, (classes[2], classes[1], classes[0]))
    packets(arrived, 2)
    packets(arrived, 1)
    mean = group_mean(64)
    sixth = dot(mean[:48, :96], gathered(1))
    fifth = gathered(2).astype(jnp.float32)
    for i in range(3):
        group = slice(i * 16, i * 16 + 16)
        forward((fifth[group], sixth[group]), pmid.at[0, i])

    def to_plane(count):
        for e, t in enumerate(plane):
            send(pmid.at[0, pl.ds(0, count)], pmid.at[e + 1, pl.ds(0, count)], PM, {"seq": t})

    pl.when(ends)(lambda: to_plane(2))
    pl.when(jnp.logical_not(ends))(lambda: to_plane(3))

    packets(arrived, 0)
    sixth = dot(mean, gathered(0)).astype(jnp.bfloat16)
    last = dot(mean[:32, :64], sixth)
    forward((last[:16], last[16:]), pfar.at[0])
    for e, t in enumerate(plane):
        send(pfar.at[0], pfar.at[e + 1], PF, {"seq": t})

    bias_prev, bias_next = open_if(has_prev), open_if(has_next)
    bias2 = [(64, open_if(ok)) for ok in groups(1)[1]]
    bias34 = [(64, open_if(ok)) for size in (2, 4) for ok in groups(size)[1]]
    near_done(arrived, 0, (0, 1, 2))
    put(0, 0, n0[0, 0], bias_prev)
    put(1, SPAN, n0[1, 0], bias_next)
    second = r2[:, 0].reshape(192, LEAF)
    low_keys = jnp.concatenate([n1[0, 0, :64], n1[1, 0], second], axis=0)
    put(0, 384, low_keys, bias_row([(64, bias_prev), (128, bias_next), *bias2]))
    high_keys = jnp.concatenate([n1[0, 0], n1[1, 0, 64:], second], axis=0)
    put(1, 384, high_keys, bias_row([(128, bias_prev), (64, bias_next), *bias2]))
    keys = jnp.concatenate([r3[:, 0].reshape(192, LEAF), r4[:, 0].reshape(192, LEAF)], axis=0)
    row = bias_row(bias34)
    put(0, 768, keys, row)
    put(1, 768, keys, row)

    biases = [(8, open_if(ok)) for pair in zip(valid5, valid6, strict=True) for ok in pair]
    row = bias_row(biases * PLANE)
    middle_blocks(arrived)
    keys = pmid[:, :, 0].reshape(MID, LEAF)
    put(0, NEAR, keys, row)
    put(1, NEAR, keys, row)
    row = bias_row([(8, open_if(ok)) for ok in valid7] * PLANE)
    arrived(pfar.at[pl.ds(0, PLANE - 1)], PF)
    keys = pfar[:, 0].reshape(FAR, LEAF)
    put(0, NEAR + MID, keys, row)
    put(1, NEAR + MID, keys, row)

    second = r2[:, 1].reshape(192, LEAF)
    middle = jnp.concatenate([r3[:, 1].reshape(192, LEAF), r4[:, 1].reshape(192, LEAF)], axis=0)
    far = [pmid[:, :, 1].reshape(MID, LEAF), pfar[:, 1].reshape(FAR, LEAF)]
    near = (
        (n0[0, 1], kv[1], n1[0, 1, :64], n1[1, 1], second, middle, *far),
        (kv[1], n0[1, 1], n1[0, 1], n1[1, 1, 64:], second, middle, *far),
    )
    later_heads = HEADS_DEV - 1 - mine_head
    pl.when(later_heads > 0)(lambda: pl.semaphore_wait(open_head, later_heads))
    for leaf in range(2):
        rows = slice(leaf * SPAN, (leaf + 1) * SPAN)
        for low in range(leaf * SPAN, (leaf + 1) * SPAN, STRIP):
            strip = scores[low : low + STRIP]
            weights = jnp.exp(strip - jnp.max(strip, axis=1, keepdims=True))
            total[low : low + STRIP] = jnp.sum(weights, axis=1, keepdims=True)
            probs[low : low + STRIP] = weights.astype(jnp.bfloat16)
        numer = dot(probs[rows], jnp.concatenate(near[leaf], axis=0))
        numer = numer / total[rows]
        rows_out = jnp.where(lane < HD, numer[:LEAF], numer[LEAF:]).astype(jnp.bfloat16)
        att[2 * leaf] = rows_out[:64]
        att[2 * leaf + 1] = rows_out[64:]
        for to in (2 * leaf, 2 * leaf + 1):
            pl.when(head != to)(lambda to=to: send(att.at[to], gath.at[head], AT, {"head": to}))

    gath[head] = att[head]
    loads[3].wait()
    arrived(gath.at[pl.ds(0, HEADS_DEV - 1)], AT)
    rows = jnp.concatenate([gath[i] for i in range(HEADS_DEV)], axis=1)
    out_ref[...] = dot(rows, w[...]).astype(jnp.bfloat16)

    for which in range(3):
        packets(sent, which)
    near_done(sent, 1, (1, 0, 2))
    middle_blocks(sent)
    sent(pfar.at[pl.ds(0, PLANE - 1)], PF)
    sent(gath.at[pl.ds(0, HEADS_DEV - 1)], AT)


def shards(queries, keys, values, out_weight):
    bf16, f32 = jnp.bfloat16, jnp.float32
    hbm = pl.BlockSpec(memory_space=pltpu.HBM)
    scratch = [
        ((SPAN, LEAF), bf16),
        ((2, SPAN, LEAF), bf16),
        ((512, 512), bf16),
        ((2, 128, LEAF), bf16),
        ((2, 64, LEAF), bf16),
        ((2, 32, LEAF), bf16),
        ((2, 16, LEAF), bf16),
        ((2, 2, LEAF, LEAF), bf16),
        ((2, 2, LEAF, LEAF), bf16),
        ((3, 2, 64, LEAF), bf16),
        ((6, 2, 32, LEAF), bf16),
        ((12, 2, 16, LEAF), bf16),
        ((PLANES, 16, LEAF), bf16),
        ((PLANE, 3, 2, 16, LEAF), bf16),
        ((PLANE, 2, 16, LEAF), bf16),
        ((2, SPAN, LEAF), bf16),
        ((ROWS, COLS), f32),
        ((ROWS, COLS), bf16),
        ((ROWS, 1), f32),
        ((HEADS_DEV, 64, LEAF), bf16),
        ((HEADS_DEV, 64, LEAF), bf16),
    ]
    return pl.pallas_call(
        kernel,
        out_shape=jax.ShapeDtypeStruct((64, 512), bf16),
        in_specs=[hbm] * 4,
        out_specs=pl.BlockSpec(memory_space=pltpu.VMEM),
        scratch_shapes=[
            *(pltpu.VMEM(shape, kind) for shape, kind in scratch),
            pltpu.SemaphoreType.DMA((4,)),
            pltpu.SemaphoreType.DMA((GROUPS,)),
            pltpu.SemaphoreType.DMA((GROUPS,)),
            pltpu.SemaphoreType.REGULAR((GROUPS - Z5,)),
            pltpu.SemaphoreType.REGULAR,
            pltpu.SemaphoreType.REGULAR,
        ],
        compiler_params=pltpu.CompilerParams(
            collective_id=0, has_side_effects=True, vmem_limit_bytes=63_400_000
        ),
    )(queries, keys, values, out_weight)


def solution(mesh):
    in_specs = (P("seq", "head"), P("seq", "head"), P("seq", "head"), P())
    out_specs = P(("seq", "head"), None)
    return jax.shard_map(shards, mesh=mesh, in_specs=in_specs, out_specs=out_specs, check_vma=False)
```

```python
import math

import jax
import jax.numpy as jnp
from jax import lax
from jax.experimental import pallas as pl
from jax.experimental.pallas import tpu as pltpu
from jax.sharding import PartitionSpec as P

MESH = pl.DeviceIdType.MESH
HD = 64
LEAF = 128
SPAN = 256
PLANE = 8
PLANES = 16
SEQ = PLANE * PLANES
HEADS_DEV = 4
NEAR, MID, FAR = 1152, 384, 128
COLS = NEAR + MID + FAR
ROWS = 4 * LEAF
STRIP = 32
N0, N1, L2, L3, L4, PM, PF, AT, Z5, Z6, Z7, GROUPS = 0, 2, 4, 7, 10, 13, 14, 15, 16, 19, 22, 24


def dot_t(a, b):
    return lax.dot_general(a, b, (((1,), (1,)), ((), ())), preferred_element_type=jnp.float32)


def dot(a, b):
    return jnp.dot(a, b, preferred_element_type=jnp.float32)


def pair_mean(rows):
    out = lax.broadcasted_iota(jnp.int32, (rows, 2 * rows), 0)
    inp = lax.broadcasted_iota(jnp.int32, (rows, 2 * rows), 1)
    return jnp.where((inp >> 1) == out, 0.5, 0.0).astype(jnp.bfloat16)


def group_mean(rows):
    out = lax.broadcasted_iota(jnp.int32, (rows, 2 * rows), 0)
    inp = lax.broadcasted_iota(jnp.int32, (rows, 2 * rows), 1)
    group = 2 * (out >> 4) + ((out >> 2) & 1)
    first = group * 16 + (out & 8) + 2 * (out & 3)
    return jnp.where((inp & ~1) == first, 0.5, 0.0).astype(jnp.bfloat16)


def open_if(valid):
    return jnp.where(valid, 0.0, -jnp.inf).astype(jnp.float32)


def bias_row(parts):
    total = sum(width for width, _ in parts)
    col = lax.broadcasted_iota(jnp.int32, (1, total), 1)
    row = jnp.zeros((1, total), jnp.float32)
    low = 0
    for width, value in parts:
        row = jnp.where((col >= low) & (col < low + width), value, row)
        low += width
    return row


def kernel(
    q_hbm, k_hbm, v_hbm, w_hbm, out_ref,
    q, kv, w, s1, s2, s3, s4, n0, n1, r2, r3, r4, zbuf, pmid, pfar,
    qm, scores, probs, total, att, gath,
    local_sem, send_sem, recv_sem, open_sem, open_near, open_head,
):
    seq = lax.axis_index("seq")
    head = lax.axis_index("head")
    z = seq // PLANE
    r = seq % PLANE

    loads = [
        pltpu.make_async_copy(k_hbm, kv.at[0], local_sem.at[0]),
        pltpu.make_async_copy(v_hbm, kv.at[1], local_sem.at[1]),
        pltpu.make_async_copy(q_hbm, q, local_sem.at[2]),
        pltpu.make_async_copy(w_hbm, w, local_sem.at[3]),
    ]
    for load in loads:
        load.start()

    def groups(size):
        index = seq // size
        odd = index % 2
        deltas = [-2, 2, 3 - 6 * odd]
        count = SEQ // size
        valid = [(index + d >= 0) & (index + d < count) for d in deltas]
        return [(index + d + count) % count for d in deltas], valid

    plane = [z * PLANE + (r ^ e) for e in (4, 5, 6, 7, 2, 3, 1)]
    heads = [head ^ e for e in (2, 1, 3)]

    zbuf[...] = jnp.zeros_like(zbuf)
    pmid[:, 2] = jnp.zeros_like(pmid[:, 2])

    @pl.when((z == 0) | (z == PLANES - 1))
    def _():
        for ref in (n0, n1, r2, r3, r4):
            ref[...] = jnp.zeros_like(ref)

    def rank(place):
        return (place >> 1 ^ place >> 2) * 2 + (place & 1)

    def tell(sem, **to):
        pl.semaphore_signal(sem, inc=1, device_id=to, device_id_type=MESH)

    barrier = pltpu.get_barrier_semaphore()
    for d in (8, 7, 9, 6, 10, 5, 11, 4, 12, 3, 13, 2, 14, 15):
        pl.when(z + d < PLANES)(lambda d=d: tell(barrier, seq=seq + d * PLANE))
    mine, mine_head = rank(r), head ^ head >> 1
    above = (z + 1 < PLANES).astype(jnp.int32)
    below = (z > 0).astype(jnp.int32)

    def greet(later, near, heads_sem):
        def chosen(a, b):
            return a < b if later else a > b

        for t in heads:
            pl.when(chosen(mine_head, t ^ t >> 1))(lambda t=t: tell(heads_sem, head=t))
        for e in range(1, PLANE):
            if e > 1:
                pl.when(chosen(mine, rank(r ^ e)))(lambda e=e: tell(near, seq=seq ^ e))
            elif later:
                tell(near, seq=seq ^ e)
        for d in (1, -1):
            for e in range(PLANE):
                place = r ^ e
                if d == 1:
                    first = jnp.logical_not((place < 2) & (r >= 2))
                else:
                    first = (r < 2) & (place >= 2)
                turn = first if later else jnp.logical_not(first)

                @pl.when((z + d >= 0) & (z + d < PLANES) & turn)
                def _(d=d, place=place):
                    tell(near, seq=(z + d) * PLANE + place)

    greet(True, barrier, barrier)

    def send(src, dst, group, to):
        pltpu.make_async_remote_copy(
            src_ref=src, dst_ref=dst, send_sem=send_sem.at[group], recv_sem=recv_sem.at[group],
            device_id=to, device_id_type=MESH,
        ).start()

    def arrived(ref, group):
        pltpu.make_async_copy(ref, ref, recv_sem.at[group]).wait()

    def sent(ref, group):
        pltpu.make_async_copy(ref, ref, send_sem.at[group]).wait()

    loads[0].wait()
    loads[1].wait()
    both = jnp.concatenate([kv[0], kv[1]], axis=1)
    mean = pair_mean(LEAF)
    level = both
    for dst, rows in ((s1, 128), (s2, 64), (s3, 32), (s4, 16)):
        level = dot(mean[:rows, : 2 * rows], level).astype(jnp.bfloat16)
        dst[0] = level[:, :128]
        dst[1] = level[:, 128:]
    last = dot(mean[:8, :16], level)
    zbuf[z] = jnp.concatenate([last[:, :128], last[:, 128:]], axis=0).astype(jnp.bfloat16)

    core = seq % 2
    inner = (r >= 2).astype(jnp.int32)
    early_beside = 2 * inner * above + (2 + 6 * inner) * below
    pl.semaphore_wait(barrier, mine - core + 1 + early_beside + z - below + mine_head)

    seventh = z // 4
    step = 3 - 6 * (seventh % 2)
    sevenths = [(seventh + 2) % 4, jnp.clip(seventh + step, 0, 3)]
    valid7 = [seventh >= 0, (seventh + step >= 0) & (seventh + step < 4)]
    low_half = z < PLANES // 2

    def existing_first(size):
        (a, b, c), (is_a, is_b, is_c) = groups(size)
        pick = lambda low, high: jnp.where(low_half, low, high)
        others, valid = [pick(b, a), c, pick(a, b)], [pick(is_b, is_a), is_c, pick(is_a, is_b)]
        return others, valid

    (sixths, valid6), (fifths, valid5) = existing_first(2 * PLANE), existing_first(PLANE)
    one = low_half.astype(jnp.int32)
    here, there = (one, 2, 1 - one), (1 - one, 2, one)
    classes = (
        (Z7, 4, sevenths, valid7, (0, 1), (0, 1)),
        (Z6, 2, sixths, valid6, here, there),
        (Z5, 1, fifths, valid5, here, there),
    )
    def each_group(ready, chosen):
        for group, size, others, valid, places, slots in chosen:
            for other, ok, i, slot in zip(others, valid, places, slots, strict=True):
                targets = [(other * size + (z % size ^ e)) * PLANE + r for e in range(size)]

                def push(targets=targets, group=group, slot=slot):
                    for t in targets:
                        send(zbuf.at[z], zbuf.at[z], group + slot, {"seq": t})

                def admit(targets=targets, group=group, slot=slot):
                    for t in targets:
                        tell(open_sem.at[group - Z5 + slot], seq=t)

                def await_open(group=group, i=i, size=size):
                    pl.semaphore_wait(open_sem.at[group - Z5 + i], size)

                ready(ok, other * size, push, admit, await_open)

    def to_lower(ok, low, push, admit, await_open):
        @pl.when(ok & (low < z))
        def _():
            push()
            admit()

    def to_higher(ok, low, push, admit, await_open):
        @pl.when(ok & (low > z))
        def _():
            await_open()
            push()

    each_group(to_lower, classes)
    greet(False, open_near, open_head)

    def packets(wait, which):
        group, size, _, valid, places, slots = classes[which]
        for ok, slot in zip(valid, slots if wait is sent else places, strict=True):
            pl.when(ok)(lambda slot=slot: wait(zbuf.at[pl.ds(0, size)], group + slot))

    def gathered(which):
        _, size, others, valid, _, _ = classes[which]
        picks = [jnp.where(ok, other, z // size) for other, ok in zip(others, valid, strict=True)]
        rows = [zbuf[pl.ds(g * size, size)].reshape(size * 16, LEAF) for g in picks]
        return jnp.concatenate(rows, axis=0)

    def forward(blocks, dst):
        for side in range(2):
            half = slice(side * 8, side * 8 + 8)
            dst[side] = jnp.concatenate([block[half] for block in blocks], axis=0).astype(jnp.bfloat16)

    ends = (z < 2) | (z >= PLANES - 2)

    def middle_blocks(wait):
        pl.when(ends)(lambda: wait(pmid.at[pl.ds(0, PLANE - 1), pl.ds(0, 2)], PM))
        pl.when(jnp.logical_not(ends))(lambda: wait(pmid.at[pl.ds(0, PLANE - 1)], PM))

    later_near = PLANE - 2 - mine + core + PLANE * (above + below) - early_beside
    pl.when(later_near > 0)(lambda: pl.semaphore_wait(open_near, later_near))

    has_prev, has_next = seq >= 1, seq + 1 < SEQ
    chain = ((L2, 1, s2, r2), (L3, 2, s3, r3), (L4, 4, s4, r4))

    @pl.when(has_next)
    def _():
        send(kv.at[:, pl.ds(LEAF, LEAF)], n0.at[0], N0, {"seq": seq + 1})
        send(s1, n1.at[0], N1, {"seq": seq + 1})

    @pl.when(has_prev)
    def _():
        send(kv.at[:, pl.ds(0, LEAF)], n0.at[1], N0 + 1, {"seq": seq - 1})
        send(s1, n1.at[1], N1 + 1, {"seq": seq - 1})

    for group, size, src, dst in chain:
        for i, (other, ok) in enumerate(zip(*groups(size), strict=True)):

            @pl.when(ok)
            def _(group=group, size=size, src=src, dst=dst, i=i, other=other):
                slot = (1, 0, 2)[i]
                for e in range(size):
                    to = other * size + (seq % size ^ e)
                    send(src, dst.at[slot * size + e], group + slot, {"seq": to})

    def near_done(wait, here, slots):
        for group, ref in ((N0, n0), (N1, n1)):
            pl.when(has_prev)(lambda group=group, ref=ref: wait(ref.at[0], group + here))
            pl.when(has_next)(lambda group=group, ref=ref: wait(ref.at[1], group + 1 - here))
        for group, size, _, dst in chain:
            for i, ok in enumerate(groups(size)[1]):
                k = slots[i]
                pl.when(ok)(lambda g=group, n=size, d=dst, k=k: wait(d.at[pl.ds(k * n, n)], g + k))

    loads[2].wait()
    lane = lax.broadcasted_iota(jnp.int32, (LEAF, LEAF), 1)
    for leaf in range(2):
        block = q[leaf * LEAF : (leaf + 1) * LEAF] * jnp.bfloat16(1.0 / math.sqrt(HD))
        qm[leaf, :LEAF] = jnp.where(lane < HD, block, jnp.bfloat16(0))
        qm[leaf, LEAF:] = jnp.where(lane < HD, jnp.bfloat16(0), block)

    def put(leaf, low, keys, bias=None):
        part = dot_t(qm[leaf], keys)
        if bias is not None:
            part = part + bias
        scores[leaf * SPAN : (leaf + 1) * SPAN, low : low + keys.shape[0]] = part

    put(0, LEAF, kv[0])
    put(1, 0, kv[0])

    each_group(to_higher, (classes[2], classes[1], classes[0]))
    packets(arrived, 2)
    packets(arrived, 1)
    mean = group_mean(64)
    sixth = dot(mean[:48, :96], gathered(1))
    fifth = gathered(2).astype(jnp.float32)
    for i in range(3):
        group = slice(i * 16, i * 16 + 16)
        forward((fifth[group], sixth[group]), pmid.at[0, i])

    def to_plane(count):
        for e, t in enumerate(plane):
            send(pmid.at[0, pl.ds(0, count)], pmid.at[e + 1, pl.ds(0, count)], PM, {"seq": t})

    pl.when(ends)(lambda: to_plane(2))
    pl.when(jnp.logical_not(ends))(lambda: to_plane(3))

    packets(arrived, 0)
    sixth = dot(mean, gathered(0)).astype(jnp.bfloat16)
    last = dot(mean[:32, :64], sixth)
    forward((last[:16], last[16:]), pfar.at[0])
    for e, t in enumerate(plane):
        send(pfar.at[0], pfar.at[e + 1], PF, {"seq": t})

    bias_prev, bias_next = open_if(has_prev), open_if(has_next)
    bias2 = [(64, open_if(ok)) for ok in groups(1)[1]]
    bias34 = [(64, open_if(ok)) for size in (2, 4) for ok in groups(size)[1]]
    near_done(arrived, 0, (0, 1, 2))
    put(0, 0, n0[0, 0], bias_prev)
    put(1, SPAN, n0[1, 0], bias_next)
    second = r2[:, 0].reshape(192, LEAF)
    low_keys = jnp.concatenate([n1[0, 0, :64], n1[1, 0], second], axis=0)
    put(0, 384, low_keys, bias_row([(64, bias_prev), (128, bias_next), *bias2]))
    high_keys = jnp.concatenate([n1[0, 0], n1[1, 0, 64:], second], axis=0)
    put(1, 384, high_keys, bias_row([(128, bias_prev), (64, bias_next), *bias2]))
    keys = jnp.concatenate([r3[:, 0].reshape(192, LEAF), r4[:, 0].reshape(192, LEAF)], axis=0)
    row = bias_row(bias34)
    put(0, 768, keys, row)
    put(1, 768, keys, row)

    biases = [(8, open_if(ok)) for pair in zip(valid5, valid6, strict=True) for ok in pair]
    row = bias_row(biases * PLANE)
    middle_blocks(arrived)
    keys = pmid[:, :, 0].reshape(MID, LEAF)
    put(0, NEAR, keys, row)
    put(1, NEAR, keys, row)
    row = bias_row([(8, open_if(ok)) for ok in valid7] * PLANE)
    arrived(pfar.at[pl.ds(0, PLANE - 1)], PF)
    keys = pfar[:, 0].reshape(FAR, LEAF)
    put(0, NEAR + MID, keys, row)
    put(1, NEAR + MID, keys, row)

    second = r2[:, 1].reshape(192, LEAF)
    middle = jnp.concatenate([r3[:, 1].reshape(192, LEAF), r4[:, 1].reshape(192, LEAF)], axis=0)
    far = [pmid[:, :, 1].reshape(MID, LEAF), pfar[:, 1].reshape(FAR, LEAF)]
    near = (
        (n0[0, 1], kv[1], n1[0, 1, :64], n1[1, 1], second, middle, *far),
        (kv[1], n0[1, 1], n1[0, 1], n1[1, 1, 64:], second, middle, *far),
    )
    later_heads = HEADS_DEV - 1 - mine_head
    pl.when(later_heads > 0)(lambda: pl.semaphore_wait(open_head, later_heads))
    for leaf in range(2):
        rows = slice(leaf * SPAN, (leaf + 1) * SPAN)
        for low in range(leaf * SPAN, (leaf + 1) * SPAN, STRIP):
            strip = scores[low : low + STRIP]
            weights = jnp.exp(strip - jnp.max(strip, axis=1, keepdims=True))
            total[low : low + STRIP] = jnp.sum(weights, axis=1, keepdims=True)
            probs[low : low + STRIP] = weights.astype(jnp.bfloat16)
        numer = dot(probs[rows], jnp.concatenate(near[leaf], axis=0))
        numer = numer / total[rows]
        rows_out = jnp.where(lane < HD, numer[:LEAF], numer[LEAF:]).astype(jnp.bfloat16)
        att[2 * leaf] = rows_out[:64]
        att[2 * leaf + 1] = rows_out[64:]
        for to in (2 * leaf, 2 * leaf + 1):
            pl.when(head != to)(lambda to=to: send(att.at[to], gath.at[head], AT, {"head": to}))

    gath[head] = att[head]
    loads[3].wait()
    arrived(gath.at[pl.ds(0, HEADS_DEV - 1)], AT)
    rows = jnp.concatenate([gath[i] for i in range(HEADS_DEV)], axis=1)
    out_ref[...] = dot(rows, w[...]).astype(jnp.bfloat16)

    for which in range(3):
        packets(sent, which)
    near_done(sent, 1, (1, 0, 2))
    middle_blocks(sent)
    sent(pfar.at[pl.ds(0, PLANE - 1)], PF)
    sent(gath.at[pl.ds(0, HEADS_DEV - 1)], AT)


def shards(queries, keys, values, out_weight):
    bf16, f32 = jnp.bfloat16, jnp.float32
    hbm = pl.BlockSpec(memory_space=pltpu.HBM)
    scratch = [
        ((SPAN, LEAF), bf16),
        ((2, SPAN, LEAF), bf16),
        ((512, 512), bf16),
        ((2, 128, LEAF), bf16),
        ((2, 64, LEAF), bf16),
        ((2, 32, LEAF), bf16),
        ((2, 16, LEAF), bf16),
        ((2, 2, LEAF, LEAF), bf16),
        ((2, 2, LEAF, LEAF), bf16),
        ((3, 2, 64, LEAF), bf16),
        ((6, 2, 32, LEAF), bf16),
        ((12, 2, 16, LEAF), bf16),
        ((PLANES, 16, LEAF), bf16),
        ((PLANE, 3, 2, 16, LEAF), bf16),
        ((PLANE, 2, 16, LEAF), bf16),
        ((2, SPAN, LEAF), bf16),
        ((ROWS, COLS), f32),
        ((ROWS, COLS), bf16),
        ((ROWS, 1), f32),
        ((HEADS_DEV, 64, LEAF), bf16),
        ((HEADS_DEV, 64, LEAF), bf16),
    ]
    return pl.pallas_call(
        kernel,
        out_shape=jax.ShapeDtypeStruct((64, 512), bf16),
        in_specs=[hbm] * 4,
        out_specs=pl.BlockSpec(memory_space=pltpu.VMEM),
        scratch_shapes=[
            *(pltpu.VMEM(shape, kind) for shape, kind in scratch),
            pltpu.SemaphoreType.DMA((4,)),
            pltpu.SemaphoreType.DMA((GROUPS,)),
            pltpu.SemaphoreType.DMA((GROUPS,)),
            pltpu.SemaphoreType.REGULAR((GROUPS - Z5,)),
            pltpu.SemaphoreType.REGULAR,
            pltpu.SemaphoreType.REGULAR,
        ],
        compiler_params=pltpu.CompilerParams(
            collective_id=0, has_side_effects=True, vmem_limit_bytes=63_400_000
        ),
    )(queries, keys, values, out_weight)


def solution(mesh):
    in_specs = (P("seq", "head"), P("seq", "head"), P("seq", "head"), P())
    out_specs = P(("seq", "head"), None)
    return jax.shard_map(shards, mesh=mesh, in_specs=in_specs, out_specs=out_specs, check_vma=False)
```

```python
import math

import jax
import jax.numpy as jnp
from jax import lax
from jax.experimental import pallas as pl
from jax.experimental.pallas import tpu as pltpu
from jax.sharding import PartitionSpec as P

MESH = pl.DeviceIdType.MESH
HD = 64
LEAF = 128
SPAN = 256
PLANE = 8
PLANES = 16
SEQ = PLANE * PLANES
HEADS_DEV = 4
NEAR, MID, FAR = 1152, 384, 128
COLS = NEAR + MID + FAR
ROWS = 4 * LEAF
STRIP = 32
N0, N1, L2, L3, L4, PM, PF, AT, Z5, Z6, Z7, GROUPS = 0, 2, 4, 7, 10, 13, 14, 15, 16, 19, 22, 24


def dot_t(a, b):
    return lax.dot_general(a, b, (((1,), (1,)), ((), ())), preferred_element_type=jnp.float32)


def dot(a, b):
    return jnp.dot(a, b, preferred_element_type=jnp.float32)


def pair_mean(rows):
    out = lax.broadcasted_iota(jnp.int32, (rows, 2 * rows), 0)
    inp = lax.broadcasted_iota(jnp.int32, (rows, 2 * rows), 1)
    return jnp.where((inp >> 1) == out, 0.5, 0.0).astype(jnp.bfloat16)


def group_mean(rows):
    out = lax.broadcasted_iota(jnp.int32, (rows, 2 * rows), 0)
    inp = lax.broadcasted_iota(jnp.int32, (rows, 2 * rows), 1)
    group = 2 * (out >> 4) + ((out >> 2) & 1)
    first = group * 16 + (out & 8) + 2 * (out & 3)
    return jnp.where((inp & ~1) == first, 0.5, 0.0).astype(jnp.bfloat16)


def open_if(valid):
    return jnp.where(valid, 0.0, -jnp.inf).astype(jnp.float32)


def bias_row(parts):
    total = sum(width for width, _ in parts)
    col = lax.broadcasted_iota(jnp.int32, (1, total), 1)
    row = jnp.zeros((1, total), jnp.float32)
    low = 0
    for width, value in parts:
        row = jnp.where((col >= low) & (col < low + width), value, row)
        low += width
    return row


def kernel(
    q_hbm, k_hbm, v_hbm, w_hbm, out_ref,
    q, kv, w, s1, s2, s3, s4, n0, n1, r2, r3, r4, zbuf, pmid, pfar,
    qm, scores, top, probs, total, att, gath,
    local_sem, send_sem, recv_sem, open_sem, open_near, open_head,
):
    seq = lax.axis_index("seq")
    head = lax.axis_index("head")
    z = seq // PLANE
    r = seq % PLANE

    loads = [
        pltpu.make_async_copy(k_hbm, kv.at[0], local_sem.at[0]),
        pltpu.make_async_copy(v_hbm, kv.at[1], local_sem.at[1]),
        pltpu.make_async_copy(q_hbm, q, local_sem.at[2]),
        pltpu.make_async_copy(w_hbm, w, local_sem.at[3]),
    ]
    for load in loads:
        load.start()

    def groups(size):
        index = seq // size
        odd = index % 2
        deltas = [-2, 2, 3 - 6 * odd]
        count = SEQ // size
        valid = [(index + d >= 0) & (index + d < count) for d in deltas]
        return [(index + d + count) % count for d in deltas], valid

    plane = [z * PLANE + (r ^ e) for e in (4, 5, 6, 7, 2, 3, 1)]
    heads = [head ^ e for e in (2, 1, 3)]

    zbuf[...] = jnp.zeros_like(zbuf)
    pmid[:, 2] = jnp.zeros_like(pmid[:, 2])

    @pl.when((z == 0) | (z == PLANES - 1))
    def _():
        for ref in (n0, n1, r2, r3, r4):
            ref[...] = jnp.zeros_like(ref)

    def rank(place):
        return (place >> 1 ^ place >> 2) * 2 + (place & 1)

    def tell(sem, **to):
        pl.semaphore_signal(sem, inc=1, device_id=to, device_id_type=MESH)

    barrier = pltpu.get_barrier_semaphore()
    for d in (8, 7, 9, 6, 10, 5, 11, 4, 12, 3, 13, 2, 14, 15):
        pl.when(z + d < PLANES)(lambda d=d: tell(barrier, seq=seq + d * PLANE))
    mine, mine_head = rank(r), head ^ head >> 1
    above = (z + 1 < PLANES).astype(jnp.int32)
    below = (z > 0).astype(jnp.int32)

    def greet(later, near, heads_sem):
        def chosen(a, b):
            return a < b if later else a > b

        for t in heads:
            pl.when(chosen(mine_head, t ^ t >> 1))(lambda t=t: tell(heads_sem, head=t))
        for e in range(1, PLANE):
            if e > 1:
                pl.when(chosen(mine, rank(r ^ e)))(lambda e=e: tell(near, seq=seq ^ e))
            elif later:
                tell(near, seq=seq ^ e)
        for d in (1, -1):
            for e in range(PLANE):
                place = r ^ e
                if d == 1:
                    first = jnp.logical_not((place < 2) & (r >= 2))
                else:
                    first = (r < 2) & (place >= 2)
                turn = first if later else jnp.logical_not(first)

                @pl.when((z + d >= 0) & (z + d < PLANES) & turn)
                def _(d=d, place=place):
                    tell(near, seq=(z + d) * PLANE + place)

    greet(True, barrier, barrier)

    def send(src, dst, group, to):
        pltpu.make_async_remote_copy(
            src_ref=src, dst_ref=dst, send_sem=send_sem.at[group], recv_sem=recv_sem.at[group],
            device_id=to, device_id_type=MESH,
        ).start()

    def arrived(ref, group):
        pltpu.make_async_copy(ref, ref, recv_sem.at[group]).wait()

    def sent(ref, group):
        pltpu.make_async_copy(ref, ref, send_sem.at[group]).wait()

    loads[0].wait()
    loads[1].wait()
    both = jnp.concatenate([kv[0], kv[1]], axis=1)
    mean = pair_mean(LEAF)
    level = both
    for dst, rows in ((s1, 128), (s2, 64), (s3, 32), (s4, 16)):
        level = dot(mean[:rows, : 2 * rows], level).astype(jnp.bfloat16)
        dst[0] = level[:, :128]
        dst[1] = level[:, 128:]
    last = dot(mean[:8, :16], level)
    zbuf[z] = jnp.concatenate([last[:, :128], last[:, 128:]], axis=0).astype(jnp.bfloat16)

    core = seq % 2
    inner = (r >= 2).astype(jnp.int32)
    early_beside = 2 * inner * above + (2 + 6 * inner) * below
    pl.semaphore_wait(barrier, mine - core + 1 + early_beside + z - below + mine_head)

    seventh = z // 4
    step = 3 - 6 * (seventh % 2)
    sevenths = [(seventh + 2) % 4, jnp.clip(seventh + step, 0, 3)]
    valid7 = [seventh >= 0, (seventh + step >= 0) & (seventh + step < 4)]
    low_half = z < PLANES // 2

    def existing_first(size):
        (a, b, c), (is_a, is_b, is_c) = groups(size)
        pick = lambda low, high: jnp.where(low_half, low, high)
        others, valid = [pick(b, a), c, pick(a, b)], [pick(is_b, is_a), is_c, pick(is_a, is_b)]
        return others, valid

    (sixths, valid6), (fifths, valid5) = existing_first(2 * PLANE), existing_first(PLANE)
    one = low_half.astype(jnp.int32)
    here, there = (one, 2, 1 - one), (1 - one, 2, one)
    classes = (
        (Z7, 4, sevenths, valid7, (0, 1), (0, 1)),
        (Z6, 2, sixths, valid6, here, there),
        (Z5, 1, fifths, valid5, here, there),
    )
    def each_group(ready, chosen):
        for group, size, others, valid, places, slots in chosen:
            for other, ok, i, slot in zip(others, valid, places, slots, strict=True):
                targets = [(other * size + (z % size ^ e)) * PLANE + r for e in range(size)]

                def push(targets=targets, group=group, slot=slot):
                    for t in targets:
                        send(zbuf.at[z], zbuf.at[z], group + slot, {"seq": t})

                def admit(targets=targets, group=group, slot=slot):
                    for t in targets:
                        tell(open_sem.at[group - Z5 + slot], seq=t)

                def await_open(group=group, i=i, size=size):
                    pl.semaphore_wait(open_sem.at[group - Z5 + i], size)

                ready(ok, other * size, push, admit, await_open)

    def to_lower(ok, low, push, admit, await_open):
        @pl.when(ok & (low < z))
        def _():
            push()
            admit()

    def to_higher(ok, low, push, admit, await_open):
        @pl.when(ok & (low > z))
        def _():
            await_open()
            push()

    each_group(to_lower, classes)
    greet(False, open_near, open_head)

    def packets(wait, which):
        group, size, _, valid, places, slots = classes[which]
        for ok, slot in zip(valid, slots if wait is sent else places, strict=True):
            pl.when(ok)(lambda slot=slot: wait(zbuf.at[pl.ds(0, size)], group + slot))

    def gathered(which):
        _, size, others, valid, _, _ = classes[which]
        picks = [jnp.where(ok, other, z // size) for other, ok in zip(others, valid, strict=True)]
        rows = [zbuf[pl.ds(g * size, size)].reshape(size * 16, LEAF) for g in picks]
        return jnp.concatenate(rows, axis=0)

    def forward(blocks, dst):
        for side in range(2):
            half = slice(side * 8, side * 8 + 8)
            dst[side] = jnp.concatenate([block[half] for block in blocks], axis=0).astype(jnp.bfloat16)

    ends = (z < 2) | (z >= PLANES - 2)

    def middle_blocks(wait):
        pl.when(ends)(lambda: wait(pmid.at[pl.ds(0, PLANE - 1), pl.ds(0, 2)], PM))
        pl.when(jnp.logical_not(ends))(lambda: wait(pmid.at[pl.ds(0, PLANE - 1)], PM))

    later_near = PLANE - 2 - mine + core + PLANE * (above + below) - early_beside
    pl.when(later_near > 0)(lambda: pl.semaphore_wait(open_near, later_near))

    has_prev, has_next = seq >= 1, seq + 1 < SEQ
    chain = ((L2, 1, s2, r2), (L3, 2, s3, r3), (L4, 4, s4, r4))

    @pl.when(has_next)
    def _():
        send(kv.at[:, pl.ds(LEAF, LEAF)], n0.at[0], N0, {"seq": seq + 1})
        send(s1, n1.at[0], N1, {"seq": seq + 1})

    @pl.when(has_prev)
    def _():
        send(kv.at[:, pl.ds(0, LEAF)], n0.at[1], N0 + 1, {"seq": seq - 1})
        send(s1, n1.at[1], N1 + 1, {"seq": seq - 1})

    for group, size, src, dst in chain:
        for i, (other, ok) in enumerate(zip(*groups(size), strict=True)):

            @pl.when(ok)
            def _(group=group, size=size, src=src, dst=dst, i=i, other=other):
                slot = (1, 0, 2)[i]
                for e in range(size):
                    to = other * size + (seq % size ^ e)
                    send(src, dst.at[slot * size + e], group + slot, {"seq": to})

    def near_done(wait, here, slots):
        for group, ref in ((N0, n0), (N1, n1)):
            pl.when(has_prev)(lambda group=group, ref=ref: wait(ref.at[0], group + here))
            pl.when(has_next)(lambda group=group, ref=ref: wait(ref.at[1], group + 1 - here))
        for group, size, _, dst in chain:
            for i, ok in enumerate(groups(size)[1]):
                k = slots[i]
                pl.when(ok)(lambda g=group, n=size, d=dst, k=k: wait(d.at[pl.ds(k * n, n)], g + k))

    loads[2].wait()
    lane = lax.broadcasted_iota(jnp.int32, (LEAF, LEAF), 1)
    for leaf in range(2):
        block = q[leaf * LEAF : (leaf + 1) * LEAF] * jnp.bfloat16(1.0 / math.sqrt(HD))
        qm[leaf, :LEAF] = jnp.where(lane < HD, block, jnp.bfloat16(0))
        qm[leaf, LEAF:] = jnp.where(lane < HD, jnp.bfloat16(0), block)

    def put(leaf, low, keys, bias=None):
        part = dot_t(qm[leaf], keys)
        if bias is not None:
            part = part + bias
        scores[leaf * SPAN : (leaf + 1) * SPAN, low : low + keys.shape[0]] = part

    put(0, LEAF, kv[0])
    put(1, 0, kv[0])

    each_group(to_higher, (classes[2], classes[1], classes[0]))
    packets(arrived, 2)
    packets(arrived, 1)
    mean = group_mean(64)
    sixth = dot(mean[:48, :96], gathered(1))
    fifth = gathered(2).astype(jnp.float32)
    for i in range(3):
        group = slice(i * 16, i * 16 + 16)
        forward((fifth[group], sixth[group]), pmid.at[0, i])

    def to_plane(count):
        for e, t in enumerate(plane):
            send(pmid.at[0, pl.ds(0, count)], pmid.at[e + 1, pl.ds(0, count)], PM, {"seq": t})

    pl.when(ends)(lambda: to_plane(2))
    pl.when(jnp.logical_not(ends))(lambda: to_plane(3))

    packets(arrived, 0)
    sixth = dot(mean, gathered(0)).astype(jnp.bfloat16)
    last = dot(mean[:32, :64], sixth)
    forward((last[:16], last[16:]), pfar.at[0])
    for e, t in enumerate(plane):
        send(pfar.at[0], pfar.at[e + 1], PF, {"seq": t})

    bias_prev, bias_next = open_if(has_prev), open_if(has_next)
    bias2 = [(64, open_if(ok)) for ok in groups(1)[1]]
    bias34 = [(64, open_if(ok)) for size in (2, 4) for ok in groups(size)[1]]
    near_done(arrived, 0, (0, 1, 2))
    put(0, 0, n0[0, 0], bias_prev)
    put(1, SPAN, n0[1, 0], bias_next)
    second = r2[:, 0].reshape(192, LEAF)
    low_keys = jnp.concatenate([n1[0, 0, :64], n1[1, 0], second], axis=0)
    put(0, 384, low_keys, bias_row([(64, bias_prev), (128, bias_next), *bias2]))
    high_keys = jnp.concatenate([n1[0, 0], n1[1, 0, 64:], second], axis=0)
    put(1, 384, high_keys, bias_row([(128, bias_prev), (64, bias_next), *bias2]))
    keys = jnp.concatenate([r3[:, 0].reshape(192, LEAF), r4[:, 0].reshape(192, LEAF)], axis=0)
    row = bias_row(bias34)
    put(0, 768, keys, row)
    put(1, 768, keys, row)

    biases = [(8, open_if(ok)) for pair in zip(valid5, valid6, strict=True) for ok in pair]
    row = bias_row(biases * PLANE)
    middle_blocks(arrived)
    keys = pmid[:, :, 0].reshape(MID, LEAF)
    put(0, NEAR, keys, row)
    put(1, NEAR, keys, row)
    for low in range(0, ROWS, STRIP):
        parts = [scores[low : low + STRIP, at : at + LEAF] for at in range(0, NEAR + MID, LEAF)]
        while len(parts) > 1:
            parts = [jnp.maximum(*parts[i : i + 2]) if i + 1 < len(parts) else parts[i] for i in range(0, len(parts), 2)]
        top[low : low + STRIP] = parts[0]
    row = bias_row([(8, open_if(ok)) for ok in valid7] * PLANE)
    arrived(pfar.at[pl.ds(0, PLANE - 1)], PF)
    keys = pfar[:, 0].reshape(FAR, LEAF)

    second = r2[:, 1].reshape(192, LEAF)
    middle = jnp.concatenate([r3[:, 1].reshape(192, LEAF), r4[:, 1].reshape(192, LEAF)], axis=0)
    far = [pmid[:, :, 1].reshape(MID, LEAF), pfar[:, 1].reshape(FAR, LEAF)]
    near = (
        (n0[0, 1], kv[1], n1[0, 1, :64], n1[1, 1], second, middle, *far),
        (kv[1], n0[1, 1], n1[0, 1], n1[1, 1, 64:], second, middle, *far),
    )
    later_heads = HEADS_DEV - 1 - mine_head
    pl.when(later_heads > 0)(lambda: pl.semaphore_wait(open_head, later_heads))
    for leaf in range(2):
        put(leaf, NEAR + MID, keys, row)
        rows = slice(leaf * SPAN, (leaf + 1) * SPAN)
        for low in range(leaf * SPAN, (leaf + 1) * SPAN, STRIP):
            strip = scores[low : low + STRIP]
            highest = jnp.maximum(top[low : low + STRIP], strip[:, NEAR + MID :])
            weights = jnp.exp(strip - jnp.max(highest, axis=1, keepdims=True))
            total[low : low + STRIP] = jnp.sum(weights, axis=1, keepdims=True)
            probs[low : low + STRIP] = weights.astype(jnp.bfloat16)
        numer = dot(probs[rows], jnp.concatenate(near[leaf], axis=0))
        numer = numer / total[rows]
        rows_out = jnp.where(lane < HD, numer[:LEAF], numer[LEAF:]).astype(jnp.bfloat16)
        att[2 * leaf] = rows_out[:64]
        att[2 * leaf + 1] = rows_out[64:]
        for to in (2 * leaf, 2 * leaf + 1):
            pl.when(head != to)(lambda to=to: send(att.at[to], gath.at[head], AT, {"head": to}))

    gath[head] = att[head]
    loads[3].wait()
    arrived(gath.at[pl.ds(0, HEADS_DEV - 1)], AT)
    rows = jnp.concatenate([gath[i] for i in range(HEADS_DEV)], axis=1)
    out_ref[...] = dot(rows, w[...]).astype(jnp.bfloat16)

    for which in range(3):
        packets(sent, which)
    near_done(sent, 1, (1, 0, 2))
    middle_blocks(sent)
    sent(pfar.at[pl.ds(0, PLANE - 1)], PF)
    sent(gath.at[pl.ds(0, HEADS_DEV - 1)], AT)


def shards(queries, keys, values, out_weight):
    bf16, f32 = jnp.bfloat16, jnp.float32
    hbm = pl.BlockSpec(memory_space=pltpu.HBM)
    scratch = [
        ((SPAN, LEAF), bf16),
        ((2, SPAN, LEAF), bf16),
        ((512, 512), bf16),
        ((2, 128, LEAF), bf16),
        ((2, 64, LEAF), bf16),
        ((2, 32, LEAF), bf16),
        ((2, 16, LEAF), bf16),
        ((2, 2, LEAF, LEAF), bf16),
        ((2, 2, LEAF, LEAF), bf16),
        ((3, 2, 64, LEAF), bf16),
        ((6, 2, 32, LEAF), bf16),
        ((12, 2, 16, LEAF), bf16),
        ((PLANES, 16, LEAF), bf16),
        ((PLANE, 3, 2, 16, LEAF), bf16),
        ((PLANE, 2, 16, LEAF), bf16),
        ((2, SPAN, LEAF), bf16),
        ((ROWS, COLS), f32),
        ((ROWS, LEAF), f32),
        ((ROWS, COLS), bf16),
        ((ROWS, 1), f32),
        ((HEADS_DEV, 64, LEAF), bf16),
        ((HEADS_DEV, 64, LEAF), bf16),
    ]
    return pl.pallas_call(
        kernel,
        out_shape=jax.ShapeDtypeStruct((64, 512), bf16),
        in_specs=[hbm] * 4,
        out_specs=pl.BlockSpec(memory_space=pltpu.VMEM),
        scratch_shapes=[
            *(pltpu.VMEM(shape, kind) for shape, kind in scratch),
            pltpu.SemaphoreType.DMA((4,)),
            pltpu.SemaphoreType.DMA((GROUPS,)),
            pltpu.SemaphoreType.DMA((GROUPS,)),
            pltpu.SemaphoreType.REGULAR((GROUPS - Z5,)),
            pltpu.SemaphoreType.REGULAR,
            pltpu.SemaphoreType.REGULAR,
        ],
        compiler_params=pltpu.CompilerParams(
            collective_id=0, has_side_effects=True, vmem_limit_bytes=63_400_000
        ),
    )(queries, keys, values, out_weight)


def solution(mesh):
    in_specs = (P("seq", "head"), P("seq", "head"), P("seq", "head"), P())
    out_specs = P(("seq", "head"), None)
    return jax.shard_map(shards, mesh=mesh, in_specs=in_specs, out_specs=out_specs, check_vma=False)
```

```python
import math

import jax
import jax.numpy as jnp
from jax import lax
from jax.experimental import pallas as pl
from jax.experimental.pallas import tpu as pltpu
from jax.sharding import PartitionSpec as P

MESH = pl.DeviceIdType.MESH
HD = 64
LEAF = 128
SPAN = 256
PLANE = 8
PLANES = 16
SEQ = PLANE * PLANES
HEADS_DEV = 4
NEAR, MID, FAR = 1152, 384, 128
COLS = NEAR + MID + FAR
ROWS = 4 * LEAF
STRIP = 32
N0, N1, L2, L3, L4, PM, PF, AT, Z5, Z6, Z7, GROUPS = 0, 2, 4, 7, 10, 13, 14, 15, 16, 19, 22, 24


def dot_t(a, b):
    return lax.dot_general(a, b, (((1,), (1,)), ((), ())), preferred_element_type=jnp.float32)


def dot(a, b):
    return jnp.dot(a, b, preferred_element_type=jnp.float32)


def pair_mean(rows):
    out = lax.broadcasted_iota(jnp.int32, (rows, 2 * rows), 0)
    inp = lax.broadcasted_iota(jnp.int32, (rows, 2 * rows), 1)
    return jnp.where((inp >> 1) == out, 0.5, 0.0).astype(jnp.bfloat16)


def group_mean(rows):
    out = lax.broadcasted_iota(jnp.int32, (rows, 2 * rows), 0)
    inp = lax.broadcasted_iota(jnp.int32, (rows, 2 * rows), 1)
    group = 2 * (out >> 4) + ((out >> 2) & 1)
    first = group * 16 + (out & 8) + 2 * (out & 3)
    return jnp.where((inp & ~1) == first, 0.5, 0.0).astype(jnp.bfloat16)


def open_if(valid):
    return jnp.where(valid, 0.0, -jnp.inf).astype(jnp.float32)


def bias_row(parts):
    total = sum(width for width, _ in parts)
    col = lax.broadcasted_iota(jnp.int32, (1, total), 1)
    row = jnp.zeros((1, total), jnp.float32)
    low = 0
    for width, value in parts:
        row = jnp.where((col >= low) & (col < low + width), value, row)
        low += width
    return row


def kernel(
    q_hbm, k_hbm, v_hbm, w_hbm, out_ref,
    q, kv, w, s1, s2, s3, s4, n0, n1, r2, r3, r4, zbuf, pmid, pfar,
    qm, scores, probs, total, att, gath,
    local_sem, send_sem, recv_sem, open_sem, open_near, open_head,
):
    seq = lax.axis_index("seq")
    head = lax.axis_index("head")
    z = seq // PLANE
    r = seq % PLANE

    loads = [
        pltpu.make_async_copy(k_hbm, kv.at[0], local_sem.at[0]),
        pltpu.make_async_copy(v_hbm, kv.at[1], local_sem.at[1]),
        pltpu.make_async_copy(q_hbm, q, local_sem.at[2]),
        pltpu.make_async_copy(w_hbm, w, local_sem.at[3]),
    ]
    for load in loads:
        load.start()

    def groups(size):
        index = seq // size
        odd = index % 2
        deltas = [-2, 2, 3 - 6 * odd]
        count = SEQ // size
        valid = [(index + d >= 0) & (index + d < count) for d in deltas]
        return [(index + d + count) % count for d in deltas], valid

    plane = [z * PLANE + (r ^ e) for e in (4, 5, 6, 7, 2, 3, 1)]
    heads = [head ^ e for e in (2, 1, 3)]

    zbuf[...] = jnp.zeros_like(zbuf)
    pmid[:, 2] = jnp.zeros_like(pmid[:, 2])

    @pl.when((z == 0) | (z == PLANES - 1))
    def _():
        for ref in (n0, n1, r2, r3, r4):
            ref[...] = jnp.zeros_like(ref)

    def rank(place):
        return (place >> 1 ^ place >> 2) * 2 + (place & 1)

    def tell(sem, **to):
        pl.semaphore_signal(sem, inc=1, device_id=to, device_id_type=MESH)

    barrier = pltpu.get_barrier_semaphore()
    for d in (8, 7, 9, 6, 10, 5, 11, 4, 12, 3, 13, 2, 14, 15):
        pl.when(z + d < PLANES)(lambda d=d: tell(barrier, seq=seq + d * PLANE))
    mine, mine_head = rank(r), head ^ head >> 1
    above = (z + 1 < PLANES).astype(jnp.int32)
    below = (z > 0).astype(jnp.int32)

    def greet(later, near, heads_sem):
        def chosen(a, b):
            return a < b if later else a > b

        for t in heads:
            pl.when(chosen(mine_head, t ^ t >> 1))(lambda t=t: tell(heads_sem, head=t))
        for e in range(1, PLANE):
            if e > 1:
                pl.when(chosen(mine, rank(r ^ e)))(lambda e=e: tell(near, seq=seq ^ e))
            elif later:
                tell(near, seq=seq ^ e)
        for d in (1, -1):
            for e in range(PLANE):
                place = r ^ e
                if d == 1:
                    first = jnp.logical_not((place < 2) & (r >= 2))
                else:
                    first = (r < 2) & (place >= 2)
                turn = first if later else jnp.logical_not(first)

                @pl.when((z + d >= 0) & (z + d < PLANES) & turn)
                def _(d=d, place=place):
                    tell(near, seq=(z + d) * PLANE + place)

    greet(True, barrier, barrier)

    def send(src, dst, group, to):
        pltpu.make_async_remote_copy(
            src_ref=src, dst_ref=dst, send_sem=send_sem.at[group], recv_sem=recv_sem.at[group],
            device_id=to, device_id_type=MESH,
        ).start()

    def arrived(ref, group):
        pltpu.make_async_copy(ref, ref, recv_sem.at[group]).wait()

    def sent(ref, group):
        pltpu.make_async_copy(ref, ref, send_sem.at[group]).wait()

    loads[0].wait()
    loads[1].wait()
    both = jnp.concatenate([kv[0], kv[1]], axis=1)
    mean = pair_mean(LEAF)
    level = both
    for dst, rows in ((s1, 128), (s2, 64), (s3, 32), (s4, 16)):
        level = dot(mean[:rows, : 2 * rows], level).astype(jnp.bfloat16)
        dst[0] = level[:, :128]
        dst[1] = level[:, 128:]
    last = dot(mean[:8, :16], level)
    zbuf[z] = jnp.concatenate([last[:, :128], last[:, 128:]], axis=0).astype(jnp.bfloat16)

    core = seq % 2
    inner = (r >= 2).astype(jnp.int32)
    early_beside = 2 * inner * above + (2 + 6 * inner) * below
    pl.semaphore_wait(barrier, mine - core + 1 + early_beside + z - below + mine_head)

    seventh = z // 4
    step = 3 - 6 * (seventh % 2)
    sevenths = [(seventh + 2) % 4, jnp.clip(seventh + step, 0, 3)]
    valid7 = [seventh >= 0, (seventh + step >= 0) & (seventh + step < 4)]
    low_half = z < PLANES // 2

    def existing_first(size):
        (a, b, c), (is_a, is_b, is_c) = groups(size)
        pick = lambda low, high: jnp.where(low_half, low, high)
        others, valid = [pick(b, a), c, pick(a, b)], [pick(is_b, is_a), is_c, pick(is_a, is_b)]
        return others, valid

    (sixths, valid6), (fifths, valid5) = existing_first(2 * PLANE), existing_first(PLANE)
    one = low_half.astype(jnp.int32)
    here, there = (one, 2, 1 - one), (1 - one, 2, one)
    classes = (
        (Z7, 4, sevenths, valid7, (0, 1), (0, 1)),
        (Z6, 2, sixths, valid6, here, there),
        (Z5, 1, fifths, valid5, here, there),
    )
    def each_group(ready, chosen):
        for group, size, others, valid, places, slots in chosen:
            for other, ok, i, slot in zip(others, valid, places, slots, strict=True):
                targets = [(other * size + (z % size ^ e)) * PLANE + r for e in range(size)]

                def push(targets=targets, group=group, slot=slot):
                    for t in targets:
                        send(zbuf.at[z], zbuf.at[z], group + slot, {"seq": t})

                def admit(targets=targets, group=group, slot=slot):
                    for t in targets:
                        tell(open_sem.at[group - Z5 + slot], seq=t)

                def await_open(group=group, i=i, size=size):
                    pl.semaphore_wait(open_sem.at[group - Z5 + i], size)

                ready(ok, other * size, push, admit, await_open)

    def to_lower(ok, low, push, admit, await_open):
        @pl.when(ok & (low < z))
        def _():
            admit()
            push()

    def to_higher(ok, low, push, admit, await_open):
        @pl.when(ok & (low > z))
        def _():
            await_open()
            push()

    each_group(to_lower, classes)
    greet(False, open_near, open_head)

    def packets(wait, which):
        group, size, _, valid, places, slots = classes[which]
        for ok, slot in zip(valid, slots if wait is sent else places, strict=True):
            pl.when(ok)(lambda slot=slot: wait(zbuf.at[pl.ds(0, size)], group + slot))

    def gathered(which):
        _, size, others, valid, _, _ = classes[which]
        picks = [jnp.where(ok, other, z // size) for other, ok in zip(others, valid, strict=True)]
        rows = [zbuf[pl.ds(g * size, size)].reshape(size * 16, LEAF) for g in picks]
        return jnp.concatenate(rows, axis=0)

    def forward(blocks, dst):
        for side in range(2):
            half = slice(side * 8, side * 8 + 8)
            dst[side] = jnp.concatenate([block[half] for block in blocks], axis=0).astype(jnp.bfloat16)

    ends = (z < 2) | (z >= PLANES - 2)

    def middle_blocks(wait):
        pl.when(ends)(lambda: wait(pmid.at[pl.ds(0, PLANE - 1), pl.ds(0, 2)], PM))
        pl.when(jnp.logical_not(ends))(lambda: wait(pmid.at[pl.ds(0, PLANE - 1)], PM))

    later_near = PLANE - 2 - mine + core + PLANE * (above + below) - early_beside
    pl.when(later_near > 0)(lambda: pl.semaphore_wait(open_near, later_near))

    has_prev, has_next = seq >= 1, seq + 1 < SEQ
    chain = ((L2, 1, s2, r2), (L3, 2, s3, r3), (L4, 4, s4, r4))

    @pl.when(has_next)
    def _():
        send(kv.at[:, pl.ds(LEAF, LEAF)], n0.at[0], N0, {"seq": seq + 1})
        send(s1, n1.at[0], N1, {"seq": seq + 1})

    @pl.when(has_prev)
    def _():
        send(kv.at[:, pl.ds(0, LEAF)], n0.at[1], N0 + 1, {"seq": seq - 1})
        send(s1, n1.at[1], N1 + 1, {"seq": seq - 1})

    for group, size, src, dst in chain:
        for i, (other, ok) in enumerate(zip(*groups(size), strict=True)):

            @pl.when(ok)
            def _(group=group, size=size, src=src, dst=dst, i=i, other=other):
                slot = (1, 0, 2)[i]
                for e in range(size):
                    to = other * size + (seq % size ^ e)
                    send(src, dst.at[slot * size + e], group + slot, {"seq": to})

    def near_done(wait, here, slots):
        for group, ref in ((N0, n0), (N1, n1)):
            pl.when(has_prev)(lambda group=group, ref=ref: wait(ref.at[0], group + here))
            pl.when(has_next)(lambda group=group, ref=ref: wait(ref.at[1], group + 1 - here))
        for group, size, _, dst in chain:
            for i, ok in enumerate(groups(size)[1]):
                k = slots[i]
                pl.when(ok)(lambda g=group, n=size, d=dst, k=k: wait(d.at[pl.ds(k * n, n)], g + k))

    loads[2].wait()
    lane = lax.broadcasted_iota(jnp.int32, (LEAF, LEAF), 1)
    for leaf in range(2):
        block = q[leaf * LEAF : (leaf + 1) * LEAF] * jnp.bfloat16(1.0 / math.sqrt(HD))
        qm[leaf, :LEAF] = jnp.where(lane < HD, block, jnp.bfloat16(0))
        qm[leaf, LEAF:] = jnp.where(lane < HD, jnp.bfloat16(0), block)

    def put(leaf, low, keys, bias=None):
        part = dot_t(qm[leaf], keys)
        if bias is not None:
            part = part + bias
        scores[leaf * SPAN : (leaf + 1) * SPAN, low : low + keys.shape[0]] = part

    put(0, LEAF, kv[0])
    put(1, 0, kv[0])

    each_group(to_higher, (classes[2], classes[1], classes[0]))
    packets(arrived, 2)
    packets(arrived, 1)
    mean = group_mean(64)
    sixth = dot(mean[:48, :96], gathered(1))
    fifth = gathered(2).astype(jnp.float32)
    for i in range(3):
        group = slice(i * 16, i * 16 + 16)
        forward((fifth[group], sixth[group]), pmid.at[0, i])

    def to_plane(count):
        for e, t in enumerate(plane):
            send(pmid.at[0, pl.ds(0, count)], pmid.at[e + 1, pl.ds(0, count)], PM, {"seq": t})

    pl.when(ends)(lambda: to_plane(2))
    pl.when(jnp.logical_not(ends))(lambda: to_plane(3))

    packets(arrived, 0)
    sixth = dot(mean, gathered(0)).astype(jnp.bfloat16)
    last = dot(mean[:32, :64], sixth)
    forward((last[:16], last[16:]), pfar.at[0])
    for e, t in enumerate(plane):
        send(pfar.at[0], pfar.at[e + 1], PF, {"seq": t})

    bias_prev, bias_next = open_if(has_prev), open_if(has_next)
    bias2 = [(64, open_if(ok)) for ok in groups(1)[1]]
    bias34 = [(64, open_if(ok)) for size in (2, 4) for ok in groups(size)[1]]
    near_done(arrived, 0, (0, 1, 2))
    put(0, 0, n0[0, 0], bias_prev)
    put(1, SPAN, n0[1, 0], bias_next)
    second = r2[:, 0].reshape(192, LEAF)
    low_keys = jnp.concatenate([n1[0, 0, :64], n1[1, 0], second], axis=0)
    put(0, 384, low_keys, bias_row([(64, bias_prev), (128, bias_next), *bias2]))
    high_keys = jnp.concatenate([n1[0, 0], n1[1, 0, 64:], second], axis=0)
    put(1, 384, high_keys, bias_row([(128, bias_prev), (64, bias_next), *bias2]))
    keys = jnp.concatenate([r3[:, 0].reshape(192, LEAF), r4[:, 0].reshape(192, LEAF)], axis=0)
    row = bias_row(bias34)
    put(0, 768, keys, row)
    put(1, 768, keys, row)

    biases = [(8, open_if(ok)) for pair in zip(valid5, valid6, strict=True) for ok in pair]
    row = bias_row(biases * PLANE)
    middle_blocks(arrived)
    keys = pmid[:, :, 0].reshape(MID, LEAF)
    put(0, NEAR, keys, row)
    put(1, NEAR, keys, row)
    row = bias_row([(8, open_if(ok)) for ok in valid7] * PLANE)
    arrived(pfar.at[pl.ds(0, PLANE - 1)], PF)
    keys = pfar[:, 0].reshape(FAR, LEAF)

    second = r2[:, 1].reshape(192, LEAF)
    middle = jnp.concatenate([r3[:, 1].reshape(192, LEAF), r4[:, 1].reshape(192, LEAF)], axis=0)
    far = [pmid[:, :, 1].reshape(MID, LEAF), pfar[:, 1].reshape(FAR, LEAF)]
    near = (
        (n0[0, 1], kv[1], n1[0, 1, :64], n1[1, 1], second, middle, *far),
        (kv[1], n0[1, 1], n1[0, 1], n1[1, 1, 64:], second, middle, *far),
    )
    later_heads = HEADS_DEV - 1 - mine_head
    pl.when(later_heads > 0)(lambda: pl.semaphore_wait(open_head, later_heads))
    for leaf in range(2):
        put(leaf, NEAR + MID, keys, row)
        rows = slice(leaf * SPAN, (leaf + 1) * SPAN)
        for low in range(leaf * SPAN, (leaf + 1) * SPAN, STRIP):
            strip = scores[low : low + STRIP]
            weights = jnp.exp(strip - jnp.max(strip, axis=1, keepdims=True))
            total[low : low + STRIP] = jnp.sum(weights, axis=1, keepdims=True)
            probs[low : low + STRIP] = weights.astype(jnp.bfloat16)
        numer = dot(probs[rows], jnp.concatenate(near[leaf], axis=0))
        numer = numer / total[rows]
        rows_out = jnp.where(lane < HD, numer[:LEAF], numer[LEAF:]).astype(jnp.bfloat16)
        att[2 * leaf] = rows_out[:64]
        att[2 * leaf + 1] = rows_out[64:]
        for to in (2 * leaf, 2 * leaf + 1):
            pl.when(head != to)(lambda to=to: send(att.at[to], gath.at[head], AT, {"head": to}))

    gath[head] = att[head]
    loads[3].wait()
    arrived(gath.at[pl.ds(0, HEADS_DEV - 1)], AT)
    rows = jnp.concatenate([gath[i] for i in range(HEADS_DEV)], axis=1)
    out_ref[...] = dot(rows, w[...]).astype(jnp.bfloat16)

    for which in range(3):
        packets(sent, which)
    near_done(sent, 1, (1, 0, 2))
    middle_blocks(sent)
    sent(pfar.at[pl.ds(0, PLANE - 1)], PF)
    sent(gath.at[pl.ds(0, HEADS_DEV - 1)], AT)


def shards(queries, keys, values, out_weight):
    bf16, f32 = jnp.bfloat16, jnp.float32
    hbm = pl.BlockSpec(memory_space=pltpu.HBM)
    scratch = [
        ((SPAN, LEAF), bf16),
        ((2, SPAN, LEAF), bf16),
        ((512, 512), bf16),
        ((2, 128, LEAF), bf16),
        ((2, 64, LEAF), bf16),
        ((2, 32, LEAF), bf16),
        ((2, 16, LEAF), bf16),
        ((2, 2, LEAF, LEAF), bf16),
        ((2, 2, LEAF, LEAF), bf16),
        ((3, 2, 64, LEAF), bf16),
        ((6, 2, 32, LEAF), bf16),
        ((12, 2, 16, LEAF), bf16),
        ((PLANES, 16, LEAF), bf16),
        ((PLANE, 3, 2, 16, LEAF), bf16),
        ((PLANE, 2, 16, LEAF), bf16),
        ((2, SPAN, LEAF), bf16),
        ((ROWS, COLS), f32),
        ((ROWS, COLS), bf16),
        ((ROWS, 1), f32),
        ((HEADS_DEV, 64, LEAF), bf16),
        ((HEADS_DEV, 64, LEAF), bf16),
    ]
    return pl.pallas_call(
        kernel,
        out_shape=jax.ShapeDtypeStruct((64, 512), bf16),
        in_specs=[hbm] * 4,
        out_specs=pl.BlockSpec(memory_space=pltpu.VMEM),
        scratch_shapes=[
            *(pltpu.VMEM(shape, kind) for shape, kind in scratch),
            pltpu.SemaphoreType.DMA((4,)),
            pltpu.SemaphoreType.DMA((GROUPS,)),
            pltpu.SemaphoreType.DMA((GROUPS,)),
            pltpu.SemaphoreType.REGULAR((GROUPS - Z5,)),
            pltpu.SemaphoreType.REGULAR,
            pltpu.SemaphoreType.REGULAR,
        ],
        compiler_params=pltpu.CompilerParams(
            collective_id=0, has_side_effects=True, vmem_limit_bytes=63_400_000
        ),
    )(queries, keys, values, out_weight)


def solution(mesh):
    in_specs = (P("seq", "head"), P("seq", "head"), P("seq", "head"), P())
    out_specs = P(("seq", "head"), None)
    return jax.shard_map(shards, mesh=mesh, in_specs=in_specs, out_specs=out_specs, check_vma=False)
```
